128 devices in a mesh: atom: 32 (over y, x, core), pair: 4 (over z).
Axes of the slice: x: 4, y: 4, z: 4, core: 2. Of those that a mesh axis runs over, the one named last changes fastest.
Arguments:
- atoms: bfloat16 [1048576, 128], P(('atom', 'pair')), may hold values from -6 to 6
- pair_bias: bfloat16 [1048576, 512], P(('atom', 'pair')), may hold values from -8 to 250
- key_offsets: int32 [32768], P(('atom', 'pair')), may hold values from -64 to -32
- atom_mask: int32 [1048576], P(('atom', 'pair')), may hold values 0 or 1
- atom_token: int32 [1048576], P(('atom', 'pair')), may hold values from 0 to 131071, as said below
- norm_gain: float32 [128], replicated, may hold values from 0.25 to 1.75
- w_query: bfloat16 [128, 128], replicated, may hold values from -0.5 to 0.5
- w_key: bfloat16 [128, 128], replicated, may hold values from -0.5 to 0.5
- w_value: bfloat16 [128, 128], replicated, may hold values from -0.5 to 0.5
- w_gate: bfloat16 [128, 128], replicated, may hold values from -0.5 to 0.5
- w_out: bfloat16 [128, 128], replicated, may hold values from -0.5 to 0.5
- trans_gain: float32 [128], replicated, may hold values from 0.25 to 1.75
- w_ff_gate: bfloat16 [128, 256], replicated, may hold values from -0.5 to 0.5
- w_ff_up: bfloat16 [128, 256], replicated, may hold values from -0.5 to 0.5
- w_ff_down: bfloat16 [256, 128], replicated, may hold values from -0.375 to 0.375
- w_pool: bfloat16 [128, 384], replicated, may hold values from -0.5 to 0.5
Outputs:
- atom_out: bfloat16 [1048576, 128], P(('atom', 'pair'))
- pooled: float32 [131072, 384], P(('atom', 'pair'))
The draws below stay inside these ranges and needn't reach their ends.
Inputs may be any that keep to these rules, and one draw needn't show every extreme that they name: `atom_token`: never falls along the atoms; every token has one or more atoms; for k > 0 the first atom of token 1024 * k lies 1 to 2048 atoms before atom 8192 * k, and a distance of 2048 occurs.
All inputs are finite; a program needn't handle non-finite values. No bound on the sum of `atom_mask` on one device may be relied on, other than what follows from the above.
Results may differ from the reference program's by a relative error of at most 0.013.
Values may be sent and summed in bfloat16 or wider, within the bound.
A program may use at most 128 MiB of HBM per device.

```python
import math
import jax
import jax.numpy as jnp
from jax import lax

C_ATOM = 128
HEADS = 4
TRANS_HIDDEN = 256
C_TOKEN = 384
QUERY_BLOCK = 32
KEY_WINDOW = 128
ATOM_DEV = 8192
REACH = 64
TOK_DEV = 1024
DRIFT = 2048
ATOMS = 1048576
TOKENS = 131072
QBLOCKS = 32768


def draw_atom_token(key, part):
    key = jax.random.fold_in(key, 7)
    shift_key, cut_key = jax.random.split(key)
    block_count = ATOMS // ATOM_DEV
    random_drift = jax.random.randint(shift_key, (block_count + 1,), 1, DRIFT + 1)
    boundary = jnp.arange(block_count + 1, dtype=jnp.int32)
    drifted = jnp.where((boundary == 1) | (boundary == block_count - 1), DRIFT, random_drift)
    drifted = jnp.where((boundary == 0) | (boundary == block_count), 0, drifted)
    starts = (boundary * ATOM_DEV - drifted).astype(jnp.int32)
    span_rows = ATOM_DEV + 2 * DRIFT
    block_lengths = starts[1:] - starts[:-1]

    def block_table(block_key, block_length):
        scores = jax.random.permutation(block_key, span_rows - 1).astype(jnp.int32)
        positions = jnp.arange(1, span_rows, dtype=jnp.int32)
        scores = jnp.where(positions < block_length, scores, span_rows + positions)
        ignored, chosen = lax.top_k(-scores, TOK_DEV - 1)
        cut_marks = jnp.zeros((span_rows,), jnp.int32).at[positions[chosen]].set(1)
        return jnp.cumsum(cut_marks).astype(jnp.int32)
    tables = jax.vmap(block_table)(jax.random.split(cut_key, block_count), block_lengths)
    atom_index = jnp.arange(ATOMS, dtype=jnp.int32)
    owner_block = jnp.searchsorted(starts[1:block_count], atom_index, side='right').astype(jnp.int32)
    local_rows = atom_index - starts[owner_block]
    return (owner_block * TOK_DEV + tables[owner_block, local_rows]).astype(jnp.int32)


def draw_pair_bias(key, part):
    key = jax.random.fold_in(key, 11)
    subkeys = jax.random.split(key, 2)
    width_all = HEADS * KEY_WINDOW
    base = jnp.clip(jax.random.normal(subkeys[1], (ATOMS, width_all)), -6.0, 6.0)
    return base.astype(jnp.bfloat16)


def place_ends(values, key, smallest, high):
    extent = values.shape
    index_at = [jax.random.randint(jax.random.fold_in(key, axis), (), 0, extent[axis]) for axis in range(len(extent))]
    values = values.at[tuple(index_at)].set(smallest)
    longest = extent.index(max(extent))
    index_at[longest] = (index_at[longest] + 1) % extent[longest]
    return values.at[tuple(index_at)].set(high)


def steps_of(rng, extent, cuts, low, top_value):
    loudness, own = 1.0, jax.random.fold_in(rng, 6)
    for position, parts in cuts:
        heights = jnp.exp(jax.random.uniform(jax.random.fold_in(own, position), (parts,), jnp.float32, low / len(cuts), top_value / len(cuts)))
        loudness = loudness * jnp.repeat(heights, extent[position] // parts).reshape([-1 if axis == position else 1 for axis in range(len(extent))])
    return loudness


def normal_values(key, extent, width, bound, cuts=(), held_as=jnp.bfloat16):
    array = width * jax.random.normal(key, extent, jnp.float32)
    if cuts:
        array = array * steps_of(key, extent, cuts, -0.22, 0.18)
    return jnp.clip(array, -bound, bound).astype(held_as)


def setup_inputs(seed: int = 0) -> dict:
    key_list = jax.random.split(jax.random.key(seed), 17)
    atoms = normal_values(key_list[0], (ATOMS, C_ATOM), 1.0, 6.0, ((0, 128),))
    pair_bias = draw_pair_bias(jax.random.fold_in(key_list[16], 71), 0)
    key_offsets = place_ends(jax.random.randint(key_list[2], (QBLOCKS,), 0 - REACH, 1 - QUERY_BLOCK), jax.random.fold_in(key_list[2], 1), 0 - REACH, (1 - QUERY_BLOCK) - 1).astype(jnp.int32)
    atom_mask = place_ends((jax.random.randint(key_list[3], (ATOMS,), 0, 8) < 7).astype(jnp.int32), jax.random.fold_in(key_list[3], 1), 0, 1)
    atom_token = draw_atom_token(jax.random.fold_in(key_list[16], 71), 0)
    norm_gain = jnp.clip(1.0 + 0.15 * jax.random.normal(key_list[5], (C_ATOM,), jnp.float32), 0.25, 1.75)
    w_query = normal_values(key_list[6], (C_ATOM, C_ATOM), C_ATOM ** -0.5, 0.5)
    w_key = normal_values(key_list[7], (C_ATOM, C_ATOM), C_ATOM ** -0.5, 0.5)
    w_value = normal_values(key_list[8], (C_ATOM, C_ATOM), C_ATOM ** -0.5, 0.5)
    w_gate = normal_values(key_list[9], (C_ATOM, C_ATOM), C_ATOM ** -0.5, 0.5)
    w_out = normal_values(key_list[10], (C_ATOM, C_ATOM), C_ATOM ** -0.5, 0.5)
    trans_gain = jnp.clip(1.0 + 0.15 * jax.random.normal(key_list[11], (C_ATOM,), jnp.float32), 0.25, 1.75)
    w_ff_gate = normal_values(key_list[12], (C_ATOM, TRANS_HIDDEN), C_ATOM ** -0.5, 0.5)
    w_ff_up = normal_values(key_list[13], (C_ATOM, TRANS_HIDDEN), C_ATOM ** -0.5, 0.5)
    w_ff_down = normal_values(key_list[14], (TRANS_HIDDEN, C_ATOM), TRANS_HIDDEN ** -0.5, 0.375)
    w_pool = normal_values(key_list[15], (C_ATOM, C_TOKEN), C_ATOM ** -0.5, 0.5)
    return dict(atoms=atoms, pair_bias=pair_bias, key_offsets=key_offsets, atom_mask=atom_mask, atom_token=atom_token, norm_gain=norm_gain, w_query=w_query, w_key=w_key, w_value=w_value, w_gate=w_gate, w_out=w_out, trans_gain=trans_gain, w_ff_gate=w_ff_gate, w_ff_up=w_ff_up, w_ff_down=w_ff_down, w_pool=w_pool)


EPSILON = 1e-05
MASKED = -1000000000.0

def layer_norm(values_in, gain_vec):
    floats = values_in.astype(jnp.float32)
    center = floats - lax.optimization_barrier(jnp.mean(floats, axis=-1, keepdims=True))
    spread = lax.optimization_barrier(jnp.mean(center * center, axis=-1, keepdims=True))
    return center * lax.rsqrt(spread + EPSILON) * gain_vec.astype(jnp.float32)

def window_attention(queries, gating, pair_bias, key_offsets, kv_padded, key_live):
    query_rows, feat_width = queries.shape
    head_count = pair_bias.shape[1] // KEY_WINDOW
    head_width = feat_width // head_count
    block_count = query_rows // QUERY_BLOCK
    group_size = math.gcd(16, block_count)
    group_count = block_count // group_size
    reach = KEY_WINDOW - 2 * QUERY_BLOCK
    starts = jnp.arange(block_count, dtype=jnp.int32) * QUERY_BLOCK + reach + key_offsets.astype(jnp.int32)

    def one_block(query_blk, gate_blk, bias_blk, key_start):
        window = lax.dynamic_slice_in_dim(kv_padded, key_start, KEY_WINDOW, 0).astype(jnp.float32)
        live_keys = lax.dynamic_slice_in_dim(key_live, key_start, KEY_WINDOW, 0)
        key_part = window[:, :feat_width].reshape(KEY_WINDOW, head_count, head_width)
        value_part = window[:, feat_width:].reshape(KEY_WINDOW, head_count, head_width)
        query_part = query_blk.astype(jnp.float32).reshape(QUERY_BLOCK, head_count, head_width)
        scores = jnp.einsum('qhd,khd->qhk', query_part, key_part, precision=lax.Precision.HIGHEST)
        scores = scores + bias_blk.astype(jnp.float32).reshape(QUERY_BLOCK, head_count, KEY_WINDOW)
        scores = jnp.where(live_keys[None, None, :], scores, MASKED)
        row_max = lax.optimization_barrier(jnp.max(scores, axis=-1, keepdims=True))
        exp_scores = jnp.exp(scores - row_max)
        weights = (exp_scores / lax.optimization_barrier(jnp.sum(exp_scores, axis=-1, keepdims=True))).astype(jnp.bfloat16)
        mixed = jnp.einsum('qhk,khd->qhd', weights.astype(jnp.float32), value_part, precision=lax.Precision.HIGHEST)
        return (mixed.reshape(QUERY_BLOCK, feat_width) * gate_blk).astype(jnp.bfloat16)
    inputs = (queries.reshape(group_count, group_size, QUERY_BLOCK, feat_width), gating.reshape(group_count, group_size, QUERY_BLOCK, feat_width), pair_bias.reshape(group_count, group_size, QUERY_BLOCK, head_count * KEY_WINDOW), starts.reshape(group_count, group_size))
    outputs = lax.map(lambda group_in: jax.vmap(one_block)(*group_in), inputs)
    return outputs.reshape(query_rows, feat_width)

def pool_reference(projected, atom_token, atom_mask):
    block_rows = ATOM_DEV
    block_count = ATOMS // block_rows

    def add_block(carry, inputs):
        token_sums, token_counts = carry
        proj_block, ids_block, mask_block = inputs
        first_token = ids_block[0].astype(jnp.int32)
        local_ids = (ids_block - first_token).astype(jnp.int32)
        weight = mask_block.astype(jnp.float32)
        block_sums = jax.ops.segment_sum(proj_block.astype(jnp.float32) * weight[:, None], local_ids, num_segments=block_rows)
        block_counts = jax.ops.segment_sum(weight, local_ids, num_segments=block_rows)
        token_sums = lax.dynamic_update_slice_in_dim(token_sums, lax.dynamic_slice_in_dim(token_sums, first_token, block_rows, 0) + block_sums, first_token, 0)
        token_counts = lax.dynamic_update_slice_in_dim(token_counts, lax.dynamic_slice_in_dim(token_counts, first_token, block_rows, 0) + block_counts, first_token, 0)
        return ((token_sums, token_counts), None)
    initial = (jnp.zeros((TOKENS + block_rows, C_TOKEN), jnp.float32), jnp.zeros((TOKENS + block_rows,), jnp.float32))
    carried, ignored = lax.scan(add_block, initial, (projected.reshape(block_count, block_rows, C_TOKEN), atom_token.reshape(block_count, block_rows), atom_mask.reshape(block_count, block_rows)))
    return (carried[0][:TOKENS], carried[1][:TOKENS])

def reference(atoms, pair_bias, key_offsets, atom_mask, atom_token, norm_gain, w_query, w_key, w_value, w_gate, w_out, trans_gain, w_ff_gate, w_ff_up, w_ff_down, w_pool):
    reach = KEY_WINDOW - 2 * QUERY_BLOCK
    normed = layer_norm(atoms, norm_gain).astype(jnp.bfloat16)
    query_scale = 1.0 / math.sqrt(C_ATOM // HEADS)
    queries = (jnp.dot(normed, w_query, preferred_element_type=jnp.float32) * query_scale).astype(jnp.bfloat16)
    keys_values = jnp.dot(normed, jnp.concatenate([w_key, w_value], axis=1), preferred_element_type=jnp.float32).astype(jnp.bfloat16)
    gating = jax.nn.sigmoid(jnp.dot(normed, w_gate, preferred_element_type=jnp.float32))
    kv_padded = jnp.pad(keys_values, ((reach, reach), (0, 0)))
    key_live = jnp.pad(atom_mask == 1, (reach, reach))
    attended = window_attention(queries, gating, pair_bias, key_offsets, kv_padded, key_live)
    updated = (atoms.astype(jnp.float32) + jnp.dot(attended, w_out, preferred_element_type=jnp.float32)).astype(jnp.bfloat16)
    second = layer_norm(updated, trans_gain).astype(jnp.bfloat16)
    hidden = (jax.nn.silu(jnp.dot(second, w_ff_gate, preferred_element_type=jnp.float32)) * jnp.dot(second, w_ff_up, preferred_element_type=jnp.float32)).astype(jnp.bfloat16)
    atom_out = (updated.astype(jnp.float32) + jnp.dot(hidden, w_ff_down, preferred_element_type=jnp.float32)).astype(jnp.bfloat16)
    projected = jax.nn.relu(jnp.dot(atom_out, w_pool, preferred_element_type=jnp.float32)).astype(jnp.bfloat16)
    token_sums, token_counts = pool_reference(projected, atom_token, atom_mask)
    pooled = token_sums / jnp.maximum(token_counts, 1.0)[:, None]
    return (atom_out, pooled)
```

```python
import functools
import math

import jax
import jax.numpy as jnp
from jax import lax
from jax.experimental import pallas as pl
from jax.experimental.pallas import tpu as pltpu
from jax.sharding import PartitionSpec as P

C_ATOM = 128
HEADS = 4
HEAD = C_ATOM // HEADS
HIDDEN = 256
C_TOKEN = 384
QUERY_BLOCK = 32
KEY_WINDOW = 128
ATOM_DEV = 8192
REACH = 64
TOK_DEV = 1024
EPSILON = 1e-05
MASKED = -1000000000.0
LIVE = 3e38

TILE = 512
BLOCKS = TILE // QUERY_BLOCK
SPAN = TILE + 2 * REACH
TILES = ATOM_DEV // TILE
WIN = 128
OWN_ROWS = TOK_DEV + WIN
ALL_ROWS = 2 * TOK_DEV + WIN
SUM_COLS = C_TOKEN + 128
PEN_OFF = 8
PEN_ROWS = ATOM_DEV // 128 + 2 * PEN_OFF
QSCALE = 1.0 / math.sqrt(HEAD)

NT = (((1,), (1,)), ((), ()))
AXES = ("atom", "pair")


def dot(a, b):
    return jnp.dot(a, b, preferred_element_type=jnp.float32)


def layer_norm(floats, gain):
    center = floats - jnp.mean(floats, axis=-1, keepdims=True)
    spread = jnp.mean(center * center, axis=-1, keepdims=True)
    return center * lax.rsqrt(spread + EPSILON) * gain


def sigmoid(x):
    return 0.5 * jnp.tanh(0.5 * x) + 0.5


def block_kernel(kind, tile_of, count, *refs):
    it = iter(refs)
    koff, tok = next(it), next(it)
    cur, prev, nxt, bias, mask, ids = (next(it) for _ in range(6))
    g1, wq, wk, wv, wg, wo, g2, wfg, wfu, wfd, wp = (next(it) for _ in range(11))
    below = above = acc_in = arrived = None
    if kind["halo"]:
        below, above = next(it), next(it)
    if kind["acc_in"]:
        acc_in = next(it)
    if kind["final"]:
        arrived = next(it)
    if kind["chain"]:
        next(it)
    out = next(it)
    acc_out = up_out = pooled = None
    if kind["final"]:
        pooled = next(it)
    else:
        acc_out = next(it)
    if kind["tail"]:
        up_out = next(it)
    k_s, v_s, pen_s, q_s, gate_s, att_s, proj_s, acc_s = (next(it) for _ in range(8))

    step = pl.program_id(0)
    tile = tile_of(step)
    base = (lax.axis_index("atom") * lax.axis_size("pair") + lax.axis_index("pair")) * TOK_DEV

    @pl.when(step == 0)
    def _():
        own = mask[...]
        pen_s[PEN_OFF : PEN_OFF + ATOM_DEV // 128, :] = jnp.where(own == 1, LIVE, MASKED)
        edge = jnp.full((PEN_OFF, 128), MASKED, jnp.float32)
        pen_s[0:PEN_OFF, :] = edge
        pen_s[PEN_ROWS - PEN_OFF :, :] = edge
        if kind["halo"]:
            low = below[REACH : REACH + 1, :].astype(jnp.float32)
            high = above[REACH : REACH + 1, :].astype(jnp.float32)
            pen_s[PEN_OFF - 1 : PEN_OFF, :] = jnp.where(low > 0.5, LIVE, MASKED)
            pen_s[PEN_ROWS - PEN_OFF : PEN_ROWS - PEN_OFF + 1, :] = jnp.where(
                high > 0.5, LIVE, MASKED
            )
        proj_s[:, C_TOKEN:] = jnp.ones((TILE, 128), jnp.bfloat16)
        if kind["acc_in"]:
            acc_s[0:OWN_ROWS, :] = acc_in[...]
            if kind["tail"]:
                acc_s[OWN_ROWS:, :] = jnp.zeros((ALL_ROWS - OWN_ROWS, SUM_COLS), jnp.float32)
        else:
            acc_s[...] = jnp.zeros(acc_s.shape, jnp.float32)

    first, last = prev[...], nxt[...]
    if kind["halo"]:
        first = jnp.where(tile == 0, below[0:REACH, :], first)
        last = jnp.where(tile == TILES - 1, above[0:REACH, :], last)
    rows = jnp.concatenate([first, cur[...], last], axis=0)
    normed = layer_norm(rows.astype(jnp.float32), g1[...]).astype(jnp.bfloat16)
    kv = dot(normed, jnp.concatenate([wk[...], wv[...]], axis=1))
    k_s[...] = kv[:, :C_ATOM]
    v_s[...] = kv[:, C_ATOM:]
    mid = normed[REACH : REACH + TILE]
    qg = dot(mid, jnp.concatenate([wq[...], wg[...]], axis=1))
    q_s[...] = (qg[:, :C_ATOM] * QSCALE).astype(jnp.bfloat16)
    gate_s[...] = sigmoid(qg[:, C_ATOM:])

    lane = lax.broadcasted_iota(jnp.int32, (1, C_ATOM), 1)
    heads = [(lane // HEAD == h) for h in range(HEADS)]
    head_ones = [m.astype(jnp.bfloat16) for m in heads]
    eye = (
        lax.broadcasted_iota(jnp.int32, (KEY_WINDOW, KEY_WINDOW), 0)
        == lax.broadcasted_iota(jnp.int32, (KEY_WINDOW, KEY_WINDOW), 1)
    ).astype(jnp.bfloat16)
    ones = jnp.ones((KEY_WINDOW, 128), jnp.bfloat16)
    for blk in range(BLOCKS):
        off = koff[tile * BLOCKS + blk]
        r0 = blk * QUERY_BLOCK
        window = pl.ds(r0 + REACH + off, KEY_WINDOW)
        keys = k_s[window, :].astype(jnp.bfloat16)
        values = v_s[window, :].astype(jnp.bfloat16)
        q = q_s[r0 : r0 + QUERY_BLOCK, :]
        stacked = jnp.concatenate([q * m for m in head_ones], axis=0)
        biases = jnp.concatenate(
            [
                bias[r0 : r0 + QUERY_BLOCK, h * KEY_WINDOW : (h + 1) * KEY_WINDOW]
                for h in range(HEADS)
            ],
            axis=0,
        )
        scores = lax.dot_general(
            jnp.concatenate([stacked, biases], axis=1),
            jnp.concatenate([keys, eye], axis=1),
            NT,
            preferred_element_type=jnp.float32,
        )
        place = tile * TILE + (r0 + PEN_OFF * 128) + off
        turn = 128 - (place & 127)
        pair = pen_s[pl.ds(place >> 7, 2), :]
        turned = pltpu.roll(pair, turn & 127, 1)
        limit = jnp.where(lane < turn, turned[0:1], turned[1:2])
        scores = jnp.minimum(scores, limit)
        top = jnp.max(scores, axis=1, keepdims=True)
        weights = jnp.exp(scores - top).astype(jnp.bfloat16)
        mixed = dot(weights, jnp.concatenate([values, ones], axis=1))
        num = mixed[0:QUERY_BLOCK, :C_ATOM]
        den = mixed[0:QUERY_BLOCK, C_ATOM:]
        for h in range(1, HEADS):
            part = mixed[h * QUERY_BLOCK : (h + 1) * QUERY_BLOCK]
            num = jnp.where(heads[h], part[:, :C_ATOM], num)
            den = jnp.where(heads[h], part[:, C_ATOM:], den)
        att_s[r0 : r0 + QUERY_BLOCK, :] = (
            num / den * gate_s[r0 : r0 + QUERY_BLOCK, :]
        ).astype(jnp.bfloat16)

    updated = (cur[...].astype(jnp.float32) + dot(att_s[...], wo[...])).astype(jnp.bfloat16)
    wide = updated.astype(jnp.float32)
    second = layer_norm(wide, g2[...]).astype(jnp.bfloat16)
    gated = dot(second, wfg[...])
    hidden = (gated * sigmoid(gated) * dot(second, wfu[...])).astype(jnp.bfloat16)
    atom_out = (wide + dot(hidden, wfd[...])).astype(jnp.bfloat16)
    out[...] = atom_out
    proj_s[:, :C_TOKEN] = jnp.maximum(dot(atom_out, wp[...]), 0.0).astype(jnp.bfloat16)

    row0 = tile * (TILE // 128)
    local = ids[pl.ds(row0, TILE // 128), :] - base
    local = jnp.where(mask[pl.ds(row0, TILE // 128), :] == 1, local, -1)
    row = jnp.concatenate([local[i : i + 1] for i in range(TILE // 128)], axis=1)
    head_tok = tok[tile * TILE] - base
    tail_tok = tok[tile * TILE + TILE - 1] - base
    start = (head_tok // 8) * 8
    slots = lax.broadcasted_iota(jnp.int32, (WIN, TILE), 0)

    def add(i, carry):
        at = pl.multiple_of(start + i * WIN, 8)
        table = (row - at == slots).astype(jnp.bfloat16)
        acc_s[pl.ds(at, WIN), :] += dot(table, proj_s[...])
        return carry

    lax.fori_loop(0, (tail_tok - start) // WIN + 1, add, 0)

    @pl.when(step == count - 1)
    def _():
        if kind["final"]:
            got = arrived[...].astype(jnp.float32)
            counts = got[:, C_TOKEN:]
            counts = counts + pltpu.roll(counts, 64, 1) + acc_s[0:TOK_DEV, C_TOKEN:]
            sums = got[:, :C_TOKEN] + acc_s[0:TOK_DEV, :C_TOKEN]
            counts = jnp.maximum(counts, 1.0)
            pooled[...] = sums / jnp.concatenate([counts] * (C_TOKEN // 128), axis=1)
        else:
            acc_out[...] = acc_s[0:OWN_ROWS, :]
        if kind["tail"]:
            up_out[:, :C_TOKEN] = acc_s[TOK_DEV : 2 * TOK_DEV, :C_TOKEN].astype(jnp.bfloat16)
            counts = acc_s[TOK_DEV : 2 * TOK_DEV, C_TOKEN:]
            high = counts.astype(jnp.bfloat16).astype(jnp.float32)
            up_out[:, C_TOKEN:] = jnp.where(lane < 64, high, counts - high).astype(jnp.bfloat16)


def run_tiles(ranges, kind, args, extra, chained):
    koff, tok, atoms, pair_bias, mask2, ids2, weights = args
    count = sum(b - a for a, b in ranges)

    def tile_of(step):
        done, tile = 0, 0
        for i, (a, b) in enumerate(ranges):
            tile = step + (a - done) if i == 0 else jnp.where(step >= done, step + (a - done), tile)
            done += b - a
        return tile

    per = TILE // REACH
    blocks = ATOM_DEV // REACH
    whole = lambda shape: pl.BlockSpec(shape, lambda t, *_: (0,) * len(shape))
    in_specs = [
        pl.BlockSpec((TILE, C_ATOM), lambda t, *_: (tile_of(t), 0)),
        pl.BlockSpec((REACH, C_ATOM), lambda t, *_: (jnp.maximum(tile_of(t) * per - 1, 0), 0)),
        pl.BlockSpec(
            (REACH, C_ATOM), lambda t, *_: (jnp.minimum(tile_of(t) * per + per, blocks - 1), 0)
        ),
        pl.BlockSpec((TILE, HEADS * KEY_WINDOW), lambda t, *_: (tile_of(t), 0)),
        whole(mask2.shape),
        whole(ids2.shape),
    ] + [whole(w.shape) for w in weights]
    operands = [koff, tok, atoms, atoms, atoms, pair_bias, mask2, ids2, *weights, *extra]
    in_specs += [whole(e.shape) for e in extra]
    aliases = {}
    if kind["chain"]:
        in_specs.append(pl.BlockSpec(memory_space=pl.ANY))
        aliases = {len(operands): 0}
        operands.append(chained)
    out_shape = [jax.ShapeDtypeStruct((ATOM_DEV, C_ATOM), jnp.bfloat16)]
    out_specs = [pl.BlockSpec((TILE, C_ATOM), lambda t, *_: (tile_of(t), 0))]
    if kind["final"]:
        out_shape.append(jax.ShapeDtypeStruct((TOK_DEV, C_TOKEN), jnp.float32))
    else:
        out_shape.append(jax.ShapeDtypeStruct((OWN_ROWS, SUM_COLS), jnp.float32))
    if kind["tail"]:
        out_shape.append(jax.ShapeDtypeStruct((TOK_DEV, SUM_COLS), jnp.bfloat16))
    out_specs += [whole(o.shape) for o in out_shape[1:]]
    return pl.pallas_call(
        functools.partial(block_kernel, kind, tile_of, count),
        grid_spec=pltpu.PrefetchScalarGridSpec(
            num_scalar_prefetch=2,
            grid=(count,),
            in_specs=in_specs,
            out_specs=out_specs,
            scratch_shapes=[
                pltpu.VMEM((SPAN, C_ATOM), jnp.float32),
                pltpu.VMEM((SPAN, C_ATOM), jnp.float32),
                pltpu.VMEM((PEN_ROWS, 128), jnp.float32),
                pltpu.VMEM((TILE, C_ATOM), jnp.bfloat16),
                pltpu.VMEM((TILE, C_ATOM), jnp.float32),
                pltpu.VMEM((TILE, C_ATOM), jnp.bfloat16),
                pltpu.VMEM((TILE, SUM_COLS), jnp.bfloat16),
                pltpu.VMEM((ALL_ROWS if kind["tail"] else OWN_ROWS, SUM_COLS), jnp.float32),
            ],
        ),
        out_shape=out_shape,
        input_output_aliases=aliases,
        compiler_params=pltpu.CompilerParams(
            dimension_semantics=("arbitrary",), vmem_limit_bytes=48 * 1024 * 1024
        ),
        cost_estimate=pl.CostEstimate(
            flops=count * TILE * 2000000, bytes_accessed=count * TILE * 1600, transcendentals=0
        ),
    )(*operands)


def moved(value, steps):
    count = lax.axis_size(AXES)
    first, last = max(0, -steps), min(count, count - steps)
    return lax.ppermute(value, AXES, [(i, i + steps) for i in range(first, last)])


def shards(
    atoms,
    pair_bias,
    key_offsets,
    atom_mask,
    atom_token,
    norm_gain,
    w_query,
    w_key,
    w_value,
    w_gate,
    w_out,
    trans_gain,
    w_ff_gate,
    w_ff_up,
    w_ff_down,
    w_pool,
):
    mask2 = atom_mask.reshape(ATOM_DEV // 128, 128)
    ids2 = atom_token.reshape(ATOM_DEV // 128, 128)
    marks = atom_mask.astype(jnp.bfloat16)

    def edge(rows, live):
        return jnp.concatenate([rows, jnp.broadcast_to(live[None], (16, 128))], axis=0)

    below = moved(edge(atoms[-REACH:], marks[-128:]), 1)
    above = moved(edge(atoms[:REACH], marks[:128]), -1)
    weights = (
        norm_gain[None],
        w_query,
        w_key,
        w_value,
        w_gate,
        w_out,
        trans_gain[None],
        w_ff_gate,
        w_ff_up,
        w_ff_down,
        w_pool,
    )
    args = (key_offsets, atom_token, atoms, pair_bias, mask2, ids2, weights)
    flags = dict(halo=False, acc_in=False, final=False, chain=False, tail=False)
    quarter = TILES // 4
    out, acc = run_tiles([(quarter, 2 * quarter)], flags, args, [], None)
    out, acc, up = run_tiles(
        [(3 * quarter, TILES)],
        {**flags, "halo": True, "acc_in": True, "chain": True, "tail": True},
        args,
        [below, above, acc],
        out,
    )
    arrived = moved(up, 1)
    out, acc = run_tiles(
        [(2 * quarter, 3 * quarter)],
        {**flags, "acc_in": True, "chain": True},
        args,
        [acc],
        out,
    )
    out, pooled = run_tiles(
        [(0, quarter)],
        {**flags, "halo": True, "acc_in": True, "chain": True, "final": True},
        args,
        [below, above, acc, arrived],
        out,
    )
    return (out, pooled)


def solution(mesh):
    rows = P(("atom", "pair"))
    wide = P(("atom", "pair"), None)
    in_specs = (wide, wide, rows, rows, rows) + (P(),) * 11
    return jax.shard_map(
        shards, mesh=mesh, in_specs=in_specs, out_specs=(wide, wide), check_vma=False
    )
```

```python
import functools
import math

import jax
import jax.numpy as jnp
from jax import lax
from jax.experimental import pallas as pl
from jax.experimental.pallas import tpu as pltpu
from jax.sharding import PartitionSpec as P

C_ATOM = 128
HEADS = 4
HEAD = C_ATOM // HEADS
C_TOKEN = 384
QUERY_BLOCK = 32
KEY_WINDOW = 128
ATOM_DEV = 8192
REACH = 64
TOK_DEV = 1024
DRIFT = 2048
EPSILON = 1e-05
MASKED = -1000000000.0
LIVE = 3e38

TILE = DRIFT
BLOCKS = TILE // QUERY_BLOCK
GROUP = 32
SPAN = TILE + 2 * REACH
TILES = ATOM_DEV // TILE
PART = 512
WIN = 128
ACC_ROWS = TOK_DEV + WIN
SUM_COLS = C_TOKEN + 128
PEN_OFF = 8
MASK_ROWS = ATOM_DEV // 128
PEN_ROWS = MASK_ROWS + 2 * PEN_OFF
QSCALE = 1.0 / math.sqrt(HEAD)

NT = (((1,), (1,)), ((), ()))
AXES = ("atom", "pair")
MESH = pl.DeviceIdType.MESH
VMEM_BYTES = 60 * 1024 * 1024


def dot(a, b):
    return jnp.dot(a, b, preferred_element_type=jnp.float32)


def layer_norm(rows, gain):
    same = lax.broadcasted_iota(jnp.int32, (C_ATOM, C_ATOM), 0) == lax.broadcasted_iota(
        jnp.int32, (C_ATOM, C_ATOM), 1
    )
    share = 1.0 / C_ATOM
    centering = jnp.where(same, 1.0 - share, -share).astype(jnp.bfloat16)
    center = dot(rows, centering)
    averaging = jnp.full((C_ATOM, C_ATOM), share, jnp.bfloat16)
    spread = dot((center * center).astype(jnp.bfloat16), averaging)
    return (center * lax.rsqrt(spread + EPSILON) * gain).astype(jnp.bfloat16)


def sigmoid(x):
    return 0.5 * jnp.tanh(0.5 * x) + 0.5


def tile_of(step):
    return jnp.where(step == 0, 1, jnp.where(step == 1, 3, jnp.where(step == 2, 2, 0)))


def here():
    return lax.axis_index("atom") * lax.axis_size("pair") + lax.axis_index("pair")


def place_of(device):
    pair = lax.axis_size("pair")
    return (device // pair, device % pair)


def attention_kernel(
    koff, cur, prev, nxt, bias, mask,
    g1, wq, wk, wv, wg, wo, g2, wfg, wfu, wfd,
    atoms_any, mask_any, marks_any,
    out, got_rows, got_marks,
    k_s, v_s, pen_s, q_s, gate_s, att_s, send_s, low, high, below, above,
    below_mask, above_mask, send_sem, recv_sem,
):
    step = pl.program_id(0)
    tile = tile_of(step)
    me = here()
    devices = lax.axis_size("atom") * lax.axis_size("pair")
    right = place_of((me + 1) % devices)
    left = place_of((me + devices - 1) % devices)

    def remote(source, target, n, device):
        return pltpu.make_async_remote_copy(
            src_ref=source,
            dst_ref=target,
            send_sem=send_sem.at[n],
            recv_sem=recv_sem.at[n],
            device_id=device,
            device_id_type=MESH,
        )

    edges = [
        remote(atoms_any.at[pl.ds(ATOM_DEV - REACH, REACH)], below, 0, right),
        remote(atoms_any.at[pl.ds(0, REACH)], above, 1, left),
        remote(mask_any.at[pl.ds(MASK_ROWS - 8, 8)], below_mask, 2, right),
        remote(mask_any.at[pl.ds(0, 8)], above_mask, 3, left),
    ]
    marks = remote(marks_any.at[pl.ds(MASK_ROWS - DRIFT // 128, DRIFT // 128)], got_marks, 4, right)
    tail = remote(send_s, got_rows, 5, right)

    @pl.when(step == 0)
    def _():
        barrier = pltpu.get_barrier_semaphore()
        for device in (left, right):
            pl.semaphore_signal(barrier, inc=1, device_id=device, device_id_type=MESH)
        pl.semaphore_wait(barrier, 2)
        for copy in edges:
            copy.start()
        marks.start()
        pen_s[PEN_OFF : PEN_OFF + MASK_ROWS, :] = jnp.where(mask[...] == 1, LIVE, MASKED)
        nothing = jnp.full((PEN_OFF, 128), MASKED, jnp.float32)
        pen_s[0:PEN_OFF, :] = nothing
        pen_s[PEN_ROWS - PEN_OFF :, :] = nothing
        low[...] = jnp.zeros((REACH, C_ATOM), jnp.bfloat16)
        high[...] = jnp.zeros((REACH, C_ATOM), jnp.bfloat16)

    @pl.when(step == 1)
    def _():
        for copy in edges:
            copy.wait()
        pen_s[0:PEN_OFF, :] = jnp.where((below_mask[...] == 1) & (me > 0), LIVE, MASKED)
        pen_s[PEN_ROWS - PEN_OFF :, :] = jnp.where(
            (above_mask[...] == 1) & (me < devices - 1), LIVE, MASKED
        )

        @pl.when(me > 0)
        def _():
            low[...] = below[...]

        @pl.when(me < devices - 1)
        def _():
            high[...] = above[...]

    first = jnp.where(tile == 0, low[...], prev[...])
    last = jnp.where(tile == TILES - 1, high[...], nxt[...])
    normed = layer_norm(jnp.concatenate([first, cur[...], last], axis=0), g1[...])
    kv = dot(normed, jnp.concatenate([wk[...], wv[...]], axis=1))
    k_s[...] = kv[:, :C_ATOM]
    v_s[...] = kv[:, C_ATOM:]
    qg = dot(normed[REACH : REACH + TILE], jnp.concatenate([wq[...], wg[...]], axis=1))
    q_s[...] = (qg[:, :C_ATOM] * QSCALE).astype(jnp.bfloat16)
    gate_s[...] = sigmoid(qg[:, C_ATOM:])

    lane = lax.broadcasted_iota(jnp.int32, (1, C_ATOM), 1)
    heads = [(lane // HEAD == h) for h in range(HEADS)]
    head_ones = [m.astype(jnp.bfloat16) for m in heads]
    eye = (
        lax.broadcasted_iota(jnp.int32, (KEY_WINDOW, KEY_WINDOW), 0)
        == lax.broadcasted_iota(jnp.int32, (KEY_WINDOW, KEY_WINDOW), 1)
    ).astype(jnp.bfloat16)
    ones = jnp.ones((KEY_WINDOW, 128), jnp.bfloat16)

    def group(g, carry):
        g0 = pl.multiple_of(g * (GROUP * QUERY_BLOCK), GROUP * QUERY_BLOCK)
        scores, limits, weights, mixes = [], [], [], []
        offs = [
            jnp.clip(koff[tile * BLOCKS + g * GROUP + blk], -REACH, -QUERY_BLOCK)
            for blk in range(GROUP)
        ]
        rows = [pl.ds(g0 + blk * QUERY_BLOCK, QUERY_BLOCK) for blk in range(GROUP)]
        windows = [
            pl.ds(g0 + (blk * QUERY_BLOCK + REACH) + offs[blk], KEY_WINDOW) for blk in range(GROUP)
        ]
        for blk in range(GROUP):
            keys = k_s[windows[blk], :].astype(jnp.bfloat16)
            q = q_s[rows[blk], :]
            stacked = jnp.concatenate([q * m for m in head_ones], axis=0)
            biases = jnp.concatenate(
                [
                    bias[rows[blk], h * KEY_WINDOW : (h + 1) * KEY_WINDOW]
                    for h in range(HEADS)
                ],
                axis=0,
            )
            scores.append(
                lax.dot_general(
                    jnp.concatenate([stacked, biases], axis=1),
                    jnp.concatenate([keys, eye], axis=1),
                    NT,
                    preferred_element_type=jnp.float32,
                )
            )
            place = tile * TILE + g0 + (blk * QUERY_BLOCK + PEN_OFF * 128) + offs[blk]
            turn = 128 - (place & 127)
            pair = pen_s[pl.ds(place >> 7, 2), :]
            turned = pltpu.roll(pair, turn & 127, 1)
            limits.append(jnp.where(lane < turn, turned[0:1], turned[1:2]))
        for blk in range(GROUP):
            held = jnp.minimum(scores[blk], limits[blk])
            top = jnp.max(held, axis=1, keepdims=True)
            weights.append(jnp.exp(held - top).astype(jnp.bfloat16))
        for blk in range(GROUP):
            values = v_s[windows[blk], :].astype(jnp.bfloat16)
            mixes.append(dot(weights[blk], jnp.concatenate([values, ones], axis=1)))
        for blk in range(GROUP):
            mixed = mixes[blk]
            num = mixed[0:QUERY_BLOCK, :C_ATOM]
            den = mixed[0:QUERY_BLOCK, C_ATOM:]
            for h in range(1, HEADS):
                part = mixed[h * QUERY_BLOCK : (h + 1) * QUERY_BLOCK]
                num = jnp.where(heads[h], part[:, :C_ATOM], num)
                den = jnp.where(heads[h], part[:, C_ATOM:], den)
            att_s[rows[blk], :] = (num / den * gate_s[rows[blk], :]).astype(jnp.bfloat16)
        return carry

    lax.fori_loop(0, BLOCKS // GROUP, group, 0)

    updated = (cur[...].astype(jnp.float32) + dot(att_s[...], wo[...])).astype(jnp.bfloat16)
    second = layer_norm(updated, g2[...])
    gated = dot(second, wfg[...])
    hidden = (gated * sigmoid(gated) * dot(second, wfu[...])).astype(jnp.bfloat16)
    atom_out = (updated.astype(jnp.float32) + dot(hidden, wfd[...])).astype(jnp.bfloat16)
    out[...] = atom_out

    @pl.when(step == 1)
    def _():
        send_s[...] = out[...]
        tail.start()

    @pl.when(step == TILES - 1)
    def _():
        marks.wait()
        tail.wait()


def attend(key_offsets, atoms, pair_bias, mask2, marks, weights):
    per = TILE // REACH
    blocks = ATOM_DEV // REACH
    whole = lambda shape: pl.BlockSpec(shape, lambda t: (0,) * len(shape))
    anywhere = pl.BlockSpec(memory_space=pl.ANY)
    tiles = lambda width: pl.BlockSpec((TILE, width), lambda t: (tile_of(t), 0))
    in_specs = [
        pl.BlockSpec(memory_space=pltpu.SMEM),
        tiles(C_ATOM),
        pl.BlockSpec((REACH, C_ATOM), lambda t: (jnp.maximum(tile_of(t) * per - 1, 0), 0)),
        pl.BlockSpec((REACH, C_ATOM), lambda t: (jnp.minimum(tile_of(t) * per + per, blocks - 1), 0)),
        tiles(HEADS * KEY_WINDOW),
        whole(mask2.shape),
        *[whole(w.shape) for w in weights],
        anywhere,
        anywhere,
        anywhere,
    ]
    mark_rows = DRIFT // 128
    return pl.pallas_call(
        attention_kernel,
        grid=(TILES,),
        in_specs=in_specs,
        out_specs=[tiles(C_ATOM), anywhere, anywhere],
        out_shape=[
            jax.ShapeDtypeStruct((ATOM_DEV, C_ATOM), jnp.bfloat16),
            jax.ShapeDtypeStruct((DRIFT, C_ATOM), jnp.bfloat16),
            jax.ShapeDtypeStruct((mark_rows, 128), jnp.int32),
        ],
        scratch_shapes=[
            pltpu.VMEM((SPAN, C_ATOM), jnp.float32),
            pltpu.VMEM((SPAN, C_ATOM), jnp.float32),
            pltpu.VMEM((PEN_ROWS, 128), jnp.float32),
            pltpu.VMEM((TILE, C_ATOM), jnp.bfloat16),
            pltpu.VMEM((TILE, C_ATOM), jnp.float32),
            pltpu.VMEM((TILE, C_ATOM), jnp.bfloat16),
            pltpu.VMEM((DRIFT, C_ATOM), jnp.bfloat16),
            *[pltpu.VMEM((REACH, C_ATOM), jnp.bfloat16) for _ in range(4)],
            pltpu.VMEM((8, 128), jnp.int32),
            pltpu.VMEM((8, 128), jnp.int32),
            pltpu.SemaphoreType.DMA((6,)),
            pltpu.SemaphoreType.DMA((6,)),
        ],
        compiler_params=pltpu.CompilerParams(
            dimension_semantics=("arbitrary",),
            vmem_limit_bytes=VMEM_BYTES,
            collective_id=0,
            has_side_effects=True,
        ),
        cost_estimate=pl.CostEstimate(
            flops=6 * 10**9, bytes_accessed=14 * 2**20, transcendentals=6 * 10**6
        ),
    )(key_offsets, atoms, atoms, atoms, pair_bias, mask2, *weights, atoms, mask2, marks)


def pool_kernel(tok, far_tok, rows, far_rows, marks, far_marks, wp, out, pooled, proj_s, acc_s):
    step = pl.program_id(0)
    base = here() * TOK_DEV

    @pl.when(step == 0)
    def _():
        proj_s[:, C_TOKEN:] = jnp.ones((TILE, 128), jnp.bfloat16)
        acc_s[...] = jnp.zeros(acc_s.shape, jnp.float32)

    def add_tile(values, mark_of, mark_row):
        proj_s[:, :C_TOKEN] = jnp.maximum(dot(values, wp[...]), 0.0).astype(jnp.bfloat16)
        slots = lax.broadcasted_iota(jnp.int32, (WIN, PART), 0)
        parts = []
        for part in range(TILE // PART):
            mark = mark_row(part)
            local = jnp.where(mark & 1 == 1, (mark >> 1) - base, -1)
            row = jnp.concatenate([local[i : i + 1] for i in range(PART // 128)], axis=1)
            start = jnp.clip((((mark_of(part * PART) >> 1) - base) >> 3) << 3, 0, TOK_DEV)
            end = jnp.minimum((mark_of(part * PART + PART - 1) >> 1) - base, TOK_DEV - 1)
            parts.append((row, start, (jnp.maximum(end - start, 0) >> 7) + 1))

        def window_sums(part, i):
            row, start, _ = parts[part]
            at = pl.multiple_of(start + i * WIN, 8)
            table = (row - at == slots).astype(jnp.bfloat16)
            return at, dot(table, proj_s[part * PART : (part + 1) * PART, :])

        for at, sums in [window_sums(part, 0) for part in range(len(parts))]:
            acc_s[pl.ds(at, WIN), :] += sums
        most = parts[0][2]
        for _, _, n in parts[1:]:
            most = jnp.maximum(most, n)

        @pl.when(most > 1)
        def _():
            for part in range(len(parts)):

                def add(i, carry, part=part):
                    at, sums = window_sums(part, i)
                    acc_s[pl.ds(at, WIN), :] += sums
                    return carry

                lax.fori_loop(1, parts[part][2], add, 0)

    per = PART // 128

    @pl.when(step < TILES)
    def _():
        out[...] = rows[...]
        add_tile(
            rows[...],
            lambda a: tok[step * TILE + a],
            lambda part: marks[pl.ds(step * (TILE // 128) + part * per, per), :],
        )

    @pl.when(step == TILES)
    def _():
        add_tile(
            far_rows[...],
            lambda a: far_tok[a],
            lambda part: far_marks[part * per : (part + 1) * per, :],
        )
        counts = jnp.maximum(acc_s[0:TOK_DEV, C_TOKEN:], 1.0)
        pooled[...] = acc_s[0:TOK_DEV, :C_TOKEN] / jnp.concatenate(
            [counts] * (C_TOKEN // 128), axis=1
        )


def pool(marks, far_marks, rows, far_rows, w_pool):
    whole = lambda shape: pl.BlockSpec(shape, lambda t, *_: (0,) * len(shape))
    tiles = pl.BlockSpec((TILE, C_ATOM), lambda t, *_: (jnp.minimum(t, TILES - 1), 0))
    return pl.pallas_call(
        pool_kernel,
        grid_spec=pltpu.PrefetchScalarGridSpec(
            num_scalar_prefetch=2,
            grid=(TILES + 1,),
            in_specs=[
                tiles,
                whole(far_rows.shape),
                whole(marks.shape),
                whole(far_marks.shape),
                whole(w_pool.shape),
            ],
            out_specs=[tiles, whole((TOK_DEV, C_TOKEN))],
            scratch_shapes=[
                pltpu.VMEM((TILE, SUM_COLS), jnp.bfloat16),
                pltpu.VMEM((ACC_ROWS, SUM_COLS), jnp.float32),
            ],
        ),
        out_shape=[
            jax.ShapeDtypeStruct((ATOM_DEV, C_ATOM), jnp.bfloat16),
            jax.ShapeDtypeStruct((TOK_DEV, C_TOKEN), jnp.float32),
        ],
        compiler_params=pltpu.CompilerParams(
            dimension_semantics=("arbitrary",), vmem_limit_bytes=VMEM_BYTES
        ),
        cost_estimate=pl.CostEstimate(
            flops=5 * 10**9, bytes_accessed=8 * 2**20, transcendentals=0
        ),
    )(marks.reshape(-1), far_marks.reshape(-1), rows, far_rows, marks, far_marks, w_pool)


def shards(
    atoms,
    pair_bias,
    key_offsets,
    atom_mask,
    atom_token,
    norm_gain,
    w_query,
    w_key,
    w_value,
    w_gate,
    w_out,
    trans_gain,
    w_ff_gate,
    w_ff_up,
    w_ff_down,
    w_pool,
):
    mask2 = atom_mask.reshape(MASK_ROWS, 128)
    marks = atom_token.reshape(MASK_ROWS, 128) * 2 + mask2
    weights = (
        norm_gain[None],
        w_query,
        w_key,
        w_value,
        w_gate,
        w_out,
        trans_gain[None],
        w_ff_gate,
        w_ff_up,
        w_ff_down,
    )
    rows, far_rows, far_marks = attend(key_offsets, atoms, pair_bias, mask2, marks, weights)
    return tuple(pool(marks, far_marks, rows, far_rows, w_pool))


def solution(mesh):
    rows = P(("atom", "pair"))
    wide = P(("atom", "pair"), None)
    in_specs = (wide, wide, rows, rows, rows) + (P(),) * 11
    return jax.shard_map(
        shards, mesh=mesh, in_specs=in_specs, out_specs=(wide, wide), check_vma=False
    )
```

```python
import functools
import math

import jax
import jax.numpy as jnp
from jax import lax
from jax.experimental import pallas as pl
from jax.experimental.pallas import tpu as pltpu
from jax.sharding import PartitionSpec as P

C_ATOM = 128
HEADS = 4
HEAD = C_ATOM // HEADS
C_TOKEN = 384
QUERY_BLOCK = 32
KEY_WINDOW = 128
ATOM_DEV = 8192
REACH = 64
TOK_DEV = 1024
DRIFT = 2048
EPSILON = 1e-05
MASKED = -1000000000.0
LIVE = 3e38

TILE = DRIFT
BLOCKS = TILE // QUERY_BLOCK
SPAN = TILE + 2 * REACH
TILES = ATOM_DEV // TILE
PART = 512
WIN = 128
ACC_ROWS = TOK_DEV + WIN
SUM_COLS = C_TOKEN + 128
PEN_OFF = 8
MASK_ROWS = ATOM_DEV // 128
FAR = DRIFT // 128
PEN_ROWS = MASK_ROWS + 2 * PEN_OFF
QSCALE = 1.0 / math.sqrt(HEAD)

NT = (((1,), (1,)), ((), ()))
AXES = ("atom", "pair")
MESH = pl.DeviceIdType.MESH
VMEM_BYTES = 60 * 1024 * 1024


def dot(a, b):
    return jnp.dot(a, b, preferred_element_type=jnp.float32)


def layer_norm(rows, gain):
    same = lax.broadcasted_iota(jnp.int32, (C_ATOM, C_ATOM), 0) == lax.broadcasted_iota(
        jnp.int32, (C_ATOM, C_ATOM), 1
    )
    share = 1.0 / C_ATOM
    centering = jnp.where(same, 1.0 - share, -share).astype(jnp.bfloat16)
    center = dot(rows, centering)
    averaging = jnp.full((C_ATOM, C_ATOM), share, jnp.bfloat16)
    spread = dot((center * center).astype(jnp.bfloat16), averaging)
    return (center * lax.rsqrt(spread + EPSILON) * gain).astype(jnp.bfloat16)


def sigmoid(x):
    return 0.5 * jnp.tanh(0.5 * x) + 0.5


def tile_of(step):
    return jnp.where(step == 0, 1, jnp.where(step == 1, 3, jnp.where(step == 2, 2, 0)))


def here():
    return lax.axis_index("atom") * lax.axis_size("pair") + lax.axis_index("pair")


def place_of(device):
    pair = lax.axis_size("pair")
    return (device // pair, device % pair)


def attention_kernel(
    koff, cur, prev, nxt, bias, mask, ids,
    g1, wq, wk, wv, wg, wo, g2, wfg, wfu, wfd,
    atoms_any, mask_any,
    out, got_rows, got_marks,
    k_s, v_s, pen_s, q_s, gate_s, att_s, send_s, low, high, below, above,
    below_mask, above_mask, marks_s, send_sem, recv_sem,
):
    step = pl.program_id(0)
    tile = tile_of(step)
    me = here()
    devices = lax.axis_size("atom") * lax.axis_size("pair")
    right = place_of((me + 1) % devices)
    left = place_of((me + devices - 1) % devices)

    def remote(source, target, n, device):
        return pltpu.make_async_remote_copy(
            src_ref=source,
            dst_ref=target,
            send_sem=send_sem.at[n],
            recv_sem=recv_sem.at[n],
            device_id=device,
            device_id_type=MESH,
        )

    ups = [
        remote(atoms_any.at[pl.ds(ATOM_DEV - REACH, REACH)], below, 0, right),
        remote(mask_any.at[pl.ds(MASK_ROWS - 8, 8)], below_mask, 2, right),
    ]
    downs = [
        remote(atoms_any.at[pl.ds(0, REACH)], above, 1, left),
        remote(mask_any.at[pl.ds(0, 8)], above_mask, 3, left),
    ]
    tails = [remote(marks_s, got_marks, 4, right), remote(send_s, got_rows, 5, right)]
    has_right, has_left = me < devices - 1, me > 0

    @pl.when(step == 0)
    def _():
        barrier = pltpu.get_barrier_semaphore()

        @pl.when(has_right)
        def _():
            pl.semaphore_signal(barrier, inc=1, device_id=right, device_id_type=MESH)

        @pl.when(has_left)
        def _():
            pl.semaphore_signal(barrier, inc=1, device_id=left, device_id_type=MESH)

        pen_s[PEN_OFF : PEN_OFF + MASK_ROWS, :] = jnp.where(mask[...] == 1, LIVE, MASKED)
        nothing = jnp.full((PEN_OFF, 128), MASKED, jnp.float32)
        pen_s[0:PEN_OFF, :] = nothing
        pen_s[PEN_ROWS - PEN_OFF :, :] = nothing
        low[...] = jnp.zeros((REACH, C_ATOM), jnp.bfloat16)
        high[...] = jnp.zeros((REACH, C_ATOM), jnp.bfloat16)
        marks_s[...] = ids[...] * 2 + mask[MASK_ROWS - FAR :, :]

    @pl.when(step == 1)
    def _():
        @pl.when(has_left)
        def _():
            for copy in ups:
                copy.wait_recv()
            low[...] = below[...]
            pen_s[0:PEN_OFF, :] = jnp.where(below_mask[...] == 1, LIVE, MASKED)
            for copy in downs:
                copy.wait_send()

        @pl.when(has_right)
        def _():
            for copy in downs:
                copy.wait_recv()
            high[...] = above[...]
            pen_s[PEN_ROWS - PEN_OFF :, :] = jnp.where(above_mask[...] == 1, LIVE, MASKED)
            for copy in ups:
                copy.wait_send()

    first = jnp.where(tile == 0, low[...], prev[...])
    last = jnp.where(tile == TILES - 1, high[...], nxt[...])
    normed = layer_norm(jnp.concatenate([first, cur[...], last], axis=0), g1[...])
    kv = dot(normed, jnp.concatenate([wk[...], wv[...]], axis=1))
    k_s[...] = kv[:, :C_ATOM]
    v_s[...] = kv[:, C_ATOM:]
    qg = dot(normed[REACH : REACH + TILE], jnp.concatenate([wq[...], wg[...]], axis=1))
    q_s[...] = (qg[:, :C_ATOM] * QSCALE).astype(jnp.bfloat16)
    gate_s[...] = sigmoid(qg[:, C_ATOM:])

    @pl.when(step == 0)
    def _():
        barrier = pltpu.get_barrier_semaphore()
        pl.semaphore_wait(barrier, has_right.astype(jnp.int32) + has_left.astype(jnp.int32))

        @pl.when(has_right)
        def _():
            for copy in ups:
                copy.start()
            tails[0].start()

        @pl.when(has_left)
        def _():
            for copy in downs:
                copy.start()

    lane = lax.broadcasted_iota(jnp.int32, (1, C_ATOM), 1)
    heads = [(lane // HEAD == h) for h in range(HEADS)]
    head_ones = [m.astype(jnp.bfloat16) for m in heads]
    eye = (
        lax.broadcasted_iota(jnp.int32, (KEY_WINDOW, KEY_WINDOW), 0)
        == lax.broadcasted_iota(jnp.int32, (KEY_WINDOW, KEY_WINDOW), 1)
    ).astype(jnp.bfloat16)
    ones = jnp.ones((KEY_WINDOW, 128), jnp.bfloat16)

    offs = [
        jnp.clip(koff[tile * BLOCKS + blk], -REACH, -QUERY_BLOCK) for blk in range(BLOCKS)
    ]
    rows = [slice(blk * QUERY_BLOCK, (blk + 1) * QUERY_BLOCK) for blk in range(BLOCKS)]
    windows = [
        pl.ds(blk * QUERY_BLOCK + REACH + offs[blk], KEY_WINDOW) for blk in range(BLOCKS)
    ]
    scores, limits, weights, mixes = {}, {}, {}, {}

    def score(blk):
        keys = k_s[windows[blk], :].astype(jnp.bfloat16)
        q = q_s[rows[blk], :]
        stacked = jnp.concatenate([q * m for m in head_ones], axis=0)
        biases = jnp.concatenate(
            [
                bias[rows[blk], h * KEY_WINDOW : (h + 1) * KEY_WINDOW]
                for h in range(HEADS)
            ],
            axis=0,
        )
        scores[blk] = lax.dot_general(
            jnp.concatenate([stacked, biases], axis=1),
            jnp.concatenate([keys, eye], axis=1),
            NT,
            preferred_element_type=jnp.float32,
        )
        place = tile * TILE + (blk * QUERY_BLOCK + PEN_OFF * 128) + offs[blk]
        turn = 128 - (place & 127)
        pair = pen_s[pl.ds(place >> 7, 2), :]
        turned = pltpu.roll(pair, turn & 127, 1)
        limits[blk] = jnp.where(lane < turn, turned[0:1], turned[1:2])

    def soften(blk):
        held = jnp.minimum(scores.pop(blk), limits.pop(blk))
        top = jnp.max(held, axis=1, keepdims=True)
        weights[blk] = jnp.exp(held - top).astype(jnp.bfloat16)

    def mix(blk):
        values = v_s[windows[blk], :].astype(jnp.bfloat16)
        mixes[blk] = dot(weights.pop(blk), jnp.concatenate([values, ones], axis=1))

    def finish(blk):
        mixed = mixes.pop(blk)
        num = mixed[0:QUERY_BLOCK, :C_ATOM]
        den = mixed[0:QUERY_BLOCK, C_ATOM:]
        for h in range(1, HEADS):
            part = mixed[h * QUERY_BLOCK : (h + 1) * QUERY_BLOCK]
            num = jnp.where(heads[h], part[:, :C_ATOM], num)
            den = jnp.where(heads[h], part[:, C_ATOM:], den)
        att_s[rows[blk], :] = (num / den * gate_s[rows[blk], :]).astype(jnp.bfloat16)

    for stage in (score, soften, mix, finish):
        for blk in range(BLOCKS):
            stage(blk)

    updated = (cur[...].astype(jnp.float32) + dot(att_s[...], wo[...])).astype(jnp.bfloat16)
    second = layer_norm(updated, g2[...])
    gated = dot(second, wfg[...])
    hidden = (gated * sigmoid(gated) * dot(second, wfu[...])).astype(jnp.bfloat16)
    atom_out = (updated.astype(jnp.float32) + dot(hidden, wfd[...])).astype(jnp.bfloat16)
    out[...] = atom_out

    @pl.when((step == 1) & has_right)
    def _():
        send_s[...] = out[...]
        tails[1].start()

    @pl.when((step == TILES - 1) & has_right)
    def _():
        for copy in tails:
            copy.wait_send()

    @pl.when((step == TILES - 1) & has_left)
    def _():
        for copy in tails:
            copy.wait_recv()


def attend(key_offsets, atoms, pair_bias, mask2, ids2, weights):
    per = TILE // REACH
    blocks = ATOM_DEV // REACH
    whole = lambda shape: pl.BlockSpec(shape, lambda t: (0,) * len(shape))
    anywhere = pl.BlockSpec(memory_space=pl.ANY)
    tiles = lambda width: pl.BlockSpec((TILE, width), lambda t: (tile_of(t), 0))
    in_specs = [
        pl.BlockSpec(memory_space=pltpu.SMEM),
        tiles(C_ATOM),
        pl.BlockSpec((REACH, C_ATOM), lambda t: (jnp.maximum(tile_of(t) * per - 1, 0), 0)),
        pl.BlockSpec((REACH, C_ATOM), lambda t: (jnp.minimum(tile_of(t) * per + per, blocks - 1), 0)),
        tiles(HEADS * KEY_WINDOW),
        whole(mask2.shape),
        pl.BlockSpec((FAR, 128), lambda t: (MASK_ROWS // FAR - 1, 0)),
        *[whole(w.shape) for w in weights],
        anywhere,
        anywhere,
    ]
    return pl.pallas_call(
        attention_kernel,
        grid=(TILES,),
        in_specs=in_specs,
        out_specs=[tiles(C_ATOM), anywhere, anywhere],
        out_shape=[
            jax.ShapeDtypeStruct((ATOM_DEV, C_ATOM), jnp.bfloat16),
            jax.ShapeDtypeStruct((DRIFT, C_ATOM), jnp.bfloat16),
            jax.ShapeDtypeStruct((FAR, 128), jnp.int32),
        ],
        scratch_shapes=[
            pltpu.VMEM((SPAN, C_ATOM), jnp.float32),
            pltpu.VMEM((SPAN, C_ATOM), jnp.float32),
            pltpu.VMEM((PEN_ROWS, 128), jnp.float32),
            pltpu.VMEM((TILE, C_ATOM), jnp.bfloat16),
            pltpu.VMEM((TILE, C_ATOM), jnp.float32),
            pltpu.VMEM((TILE, C_ATOM), jnp.bfloat16),
            pltpu.VMEM((DRIFT, C_ATOM), jnp.bfloat16),
            *[pltpu.VMEM((REACH, C_ATOM), jnp.bfloat16) for _ in range(4)],
            pltpu.VMEM((8, 128), jnp.int32),
            pltpu.VMEM((8, 128), jnp.int32),
            pltpu.VMEM((FAR, 128), jnp.int32),
            pltpu.SemaphoreType.DMA((6,)),
            pltpu.SemaphoreType.DMA((6,)),
        ],
        compiler_params=pltpu.CompilerParams(
            dimension_semantics=("arbitrary",),
            vmem_limit_bytes=VMEM_BYTES,
            collective_id=0,
            has_side_effects=True,
        ),
        cost_estimate=pl.CostEstimate(
            flops=6 * 10**9, bytes_accessed=14 * 2**20, transcendentals=6 * 10**6
        ),
    )(key_offsets, atoms, atoms, atoms, pair_bias, mask2, ids2, *weights, atoms, mask2)


def pool_kernel(
    tok, far_tok, rows, far_rows, ids, mask, far_marks, wp, out, pooled, proj_s, acc_s
):
    step = pl.program_id(0)
    me = here()
    base = me * TOK_DEV

    @pl.when(step == 0)
    def _():
        proj_s[:, C_TOKEN:] = jnp.ones((TILE, 128), jnp.bfloat16)
        acc_s[...] = jnp.zeros(acc_s.shape, jnp.float32)

    def add_tile(values, token_of, local_of):
        proj_s[:, :C_TOKEN] = jnp.maximum(dot(values, wp[...]), 0.0).astype(jnp.bfloat16)
        slots = lax.broadcasted_iota(jnp.int32, (WIN, PART), 0)
        parts = []
        for part in range(TILE // PART):
            local = local_of(part)
            row = jnp.concatenate([local[i : i + 1] for i in range(PART // 128)], axis=1)
            start = jnp.clip(((token_of(part * PART) - base) >> 3) << 3, 0, TOK_DEV)
            end = jnp.minimum(token_of(part * PART + PART - 1) - base, TOK_DEV - 1)
            parts.append((row, start, (jnp.maximum(end - start, 0) >> 7) + 1))

        def window_sums(part, i):
            row, start, _ = parts[part]
            at = pl.multiple_of(start + i * WIN, 8)
            table = (row - at == slots).astype(jnp.bfloat16)
            return at, dot(table, proj_s[part * PART : (part + 1) * PART, :])

        for at, sums in [window_sums(part, 0) for part in range(len(parts))]:
            acc_s[pl.ds(at, WIN), :] += sums
        most = parts[0][2]
        for _, _, n in parts[1:]:
            most = jnp.maximum(most, n)

        @pl.when(most > 1)
        def _():
            for part in range(len(parts)):

                def add(i, carry, part=part):
                    at, sums = window_sums(part, i)
                    acc_s[pl.ds(at, WIN), :] += sums
                    return carry

                lax.fori_loop(1, parts[part][2], add, 0)

    per = PART // 128

    @pl.when(step < TILES)
    def _():
        def local_of(part):
            at = pl.ds(step * (TILE // 128) + part * per, per)
            return jnp.where(mask[at, :] == 1, ids[at, :] - base, -1)

        out[...] = rows[...]
        add_tile(rows[...], lambda a: tok[step * TILE + a], local_of)

    @pl.when((step == TILES) & (me > 0))
    def _():
        def local_of(part):
            mark = far_marks[part * per : (part + 1) * per, :]
            return jnp.where(mark & 1 == 1, (mark >> 1) - base, -1)

        add_tile(far_rows[...], lambda a: far_tok[a] >> 1, local_of)

    @pl.when(step == TILES)
    def _():
        counts = jnp.maximum(acc_s[0:TOK_DEV, C_TOKEN:], 1.0)
        pooled[...] = acc_s[0:TOK_DEV, :C_TOKEN] / jnp.concatenate(
            [counts] * (C_TOKEN // 128), axis=1
        )


def pool(tokens, ids2, mask2, far_marks, rows, far_rows, w_pool):
    whole = lambda shape: pl.BlockSpec(shape, lambda t, *_: (0,) * len(shape))
    tiles = pl.BlockSpec((TILE, C_ATOM), lambda t, *_: (jnp.minimum(t, TILES - 1), 0))
    return pl.pallas_call(
        pool_kernel,
        grid_spec=pltpu.PrefetchScalarGridSpec(
            num_scalar_prefetch=2,
            grid=(TILES + 1,),
            in_specs=[
                tiles,
                whole(far_rows.shape),
                whole(ids2.shape),
                whole(mask2.shape),
                whole(far_marks.shape),
                whole(w_pool.shape),
            ],
            out_specs=[tiles, whole((TOK_DEV, C_TOKEN))],
            scratch_shapes=[
                pltpu.VMEM((TILE, SUM_COLS), jnp.bfloat16),
                pltpu.VMEM((ACC_ROWS, SUM_COLS), jnp.float32),
            ],
        ),
        out_shape=[
            jax.ShapeDtypeStruct((ATOM_DEV, C_ATOM), jnp.bfloat16),
            jax.ShapeDtypeStruct((TOK_DEV, C_TOKEN), jnp.float32),
        ],
        compiler_params=pltpu.CompilerParams(
            dimension_semantics=("arbitrary",), vmem_limit_bytes=VMEM_BYTES
        ),
        cost_estimate=pl.CostEstimate(
            flops=5 * 10**9, bytes_accessed=8 * 2**20, transcendentals=0
        ),
    )(tokens, far_marks.reshape(-1), rows, far_rows, ids2, mask2, far_marks, w_pool)


def shards(
    atoms,
    pair_bias,
    key_offsets,
    atom_mask,
    atom_token,
    norm_gain,
    w_query,
    w_key,
    w_value,
    w_gate,
    w_out,
    trans_gain,
    w_ff_gate,
    w_ff_up,
    w_ff_down,
    w_pool,
):
    mask2 = atom_mask.reshape(MASK_ROWS, 128)
    ids2 = atom_token.reshape(MASK_ROWS, 128)
    weights = (
        norm_gain[None],
        w_query,
        w_key,
        w_value,
        w_gate,
        w_out,
        trans_gain[None],
        w_ff_gate,
        w_ff_up,
        w_ff_down,
    )
    rows, far_rows, far_marks = attend(key_offsets, atoms, pair_bias, mask2, ids2, weights)
    return tuple(pool(atom_token, ids2, mask2, far_marks, rows, far_rows, w_pool))


def solution(mesh):
    rows = P(("atom", "pair"))
    wide = P(("atom", "pair"), None)
    in_specs = (wide, wide, rows, rows, rows) + (P(),) * 11
    return jax.shard_map(
        shards, mesh=mesh, in_specs=in_specs, out_specs=(wide, wide), check_vma=False
    )
```

```python
import functools
import math

import jax
import jax.numpy as jnp
from jax import lax
from jax.experimental import pallas as pl
from jax.experimental.pallas import tpu as pltpu
from jax.sharding import PartitionSpec as P

C_ATOM = 128
HEADS = 4
HEAD = C_ATOM // HEADS
C_TOKEN = 384
QUERY_BLOCK = 32
KEY_WINDOW = 128
ATOM_DEV = 8192
REACH = 64
TOK_DEV = 1024
DRIFT = 2048
EPSILON = 1e-05
MASKED = -1000000000.0
LIVE = 3e38

TILE = DRIFT
BLOCKS = TILE // QUERY_BLOCK
SPAN = TILE + 2 * REACH
TILES = ATOM_DEV // TILE
PART = 512
WIN = 128
ACC_ROWS = TOK_DEV + WIN
SUM_COLS = C_TOKEN + 128
PEN_OFF = 8
MASK_ROWS = ATOM_DEV // 128
FAR = DRIFT // 128
PEN_ROWS = MASK_ROWS + 2 * PEN_OFF
QSCALE = 1.0 / math.sqrt(HEAD)

NT = (((1,), (1,)), ((), ()))
AXES = ("atom", "pair")
MESH = pl.DeviceIdType.MESH
VMEM_BYTES = 60 * 1024 * 1024


def dot(a, b):
    return jnp.dot(a, b, preferred_element_type=jnp.float32)


def layer_norm(rows, gain):
    same = lax.broadcasted_iota(jnp.int32, (C_ATOM, C_ATOM), 0) == lax.broadcasted_iota(
        jnp.int32, (C_ATOM, C_ATOM), 1
    )
    share = 1.0 / C_ATOM
    centering = jnp.where(same, 1.0 - share, -share).astype(jnp.bfloat16)
    center = dot(rows, centering)
    averaging = jnp.full((C_ATOM, C_ATOM), share, jnp.bfloat16)
    spread = dot((center * center).astype(jnp.bfloat16), averaging)
    return (center * lax.rsqrt(spread + EPSILON) * gain).astype(jnp.bfloat16)


def sigmoid(x):
    return 0.5 * jnp.tanh(0.5 * x) + 0.5


def tile_of(step):
    return jnp.where(step == 0, 1, jnp.where(step == 1, 3, jnp.where(step == 2, 2, 0)))


def here():
    return lax.axis_index("atom") * lax.axis_size("pair") + lax.axis_index("pair")


def place_of(device):
    pair = lax.axis_size("pair")
    return (device // pair, device % pair)


def attention_kernel(
    koff, cur, prev, nxt, bias, mask, ids,
    g1, wq, wk, wv, wg, wo, g2, wfg, wfu, wfd,
    atoms_any, mask_any,
    out, got_rows, got_marks,
    k_s, v_s, pen_s, q_s, gate_s, att_s, send_s, low, high, below, above,
    below_mask, above_mask, marks_s, send_sem, recv_sem,
):
    step = pl.program_id(0)
    tile = tile_of(step)
    me = here()
    devices = lax.axis_size("atom") * lax.axis_size("pair")
    right = place_of((me + 1) % devices)
    left = place_of((me + devices - 1) % devices)

    def remote(source, target, n, device):
        return pltpu.make_async_remote_copy(
            src_ref=source,
            dst_ref=target,
            send_sem=send_sem.at[n],
            recv_sem=recv_sem.at[n],
            device_id=device,
            device_id_type=MESH,
        )

    ups = [
        remote(atoms_any.at[pl.ds(ATOM_DEV - REACH, REACH)], below, 0, right),
        remote(mask_any.at[pl.ds(MASK_ROWS - 8, 8)], below_mask, 2, right),
    ]
    downs = [
        remote(atoms_any.at[pl.ds(0, REACH)], above, 1, left),
        remote(mask_any.at[pl.ds(0, 8)], above_mask, 3, left),
    ]
    tails = [remote(marks_s, got_marks, 4, right), remote(send_s, got_rows, 5, right)]
    has_right, has_left = me < devices - 1, me > 0

    @pl.when(step == 0)
    def _():
        barrier = pltpu.get_barrier_semaphore()

        @pl.when(has_right)
        def _():
            pl.semaphore_signal(barrier, inc=1, device_id=right, device_id_type=MESH)

        @pl.when(has_left)
        def _():
            pl.semaphore_signal(barrier, inc=1, device_id=left, device_id_type=MESH)

        pen_s[PEN_OFF : PEN_OFF + MASK_ROWS, :] = jnp.where(mask[...] == 1, LIVE, MASKED)
        nothing = jnp.full((PEN_OFF, 128), MASKED, jnp.float32)
        pen_s[0:PEN_OFF, :] = nothing
        pen_s[PEN_ROWS - PEN_OFF :, :] = nothing
        low[...] = jnp.zeros((REACH, C_ATOM), jnp.bfloat16)
        high[...] = jnp.zeros((REACH, C_ATOM), jnp.bfloat16)
        marks_s[...] = ids[...] * 2 + mask[MASK_ROWS - FAR :, :]

    @pl.when(step == 1)
    def _():
        @pl.when(has_left)
        def _():
            for copy in ups:
                copy.wait_recv()
            low[...] = below[...]
            pen_s[0:PEN_OFF, :] = jnp.where(below_mask[...] == 1, LIVE, MASKED)
            for copy in downs:
                copy.wait_send()

        @pl.when(has_right)
        def _():
            for copy in downs:
                copy.wait_recv()
            high[...] = above[...]
            pen_s[PEN_ROWS - PEN_OFF :, :] = jnp.where(above_mask[...] == 1, LIVE, MASKED)
            for copy in ups:
                copy.wait_send()

    first = jnp.where(tile == 0, low[...], prev[...])
    last = jnp.where(tile == TILES - 1, high[...], nxt[...])
    normed = layer_norm(jnp.concatenate([first, cur[...], last], axis=0), g1[...])
    kv = dot(normed, jnp.concatenate([wk[...], wv[...]], axis=1))
    k_s[...] = kv[:, :C_ATOM]
    v_s[...] = kv[:, C_ATOM:]
    qg = dot(normed[REACH : REACH + TILE], jnp.concatenate([wq[...], wg[...]], axis=1))
    q_s[...] = (qg[:, :C_ATOM] * QSCALE).astype(jnp.bfloat16)
    gate_s[...] = sigmoid(qg[:, C_ATOM:])

    @pl.when(step == 0)
    def _():
        barrier = pltpu.get_barrier_semaphore()
        pl.semaphore_wait(barrier, has_right.astype(jnp.int32) + has_left.astype(jnp.int32))

        @pl.when(has_right)
        def _():
            for copy in ups:
                copy.start()
            tails[0].start()

        @pl.when(has_left)
        def _():
            for copy in downs:
                copy.start()

    lane = lax.broadcasted_iota(jnp.int32, (1, C_ATOM), 1)
    heads = [(lane // HEAD == h) for h in range(HEADS)]
    head_ones = [m.astype(jnp.bfloat16) for m in heads]
    eye = (
        lax.broadcasted_iota(jnp.int32, (KEY_WINDOW, KEY_WINDOW), 0)
        == lax.broadcasted_iota(jnp.int32, (KEY_WINDOW, KEY_WINDOW), 1)
    ).astype(jnp.bfloat16)
    ones = jnp.ones((KEY_WINDOW, 128), jnp.bfloat16)

    offs = [
        jnp.clip(koff[tile * BLOCKS + blk], -REACH, -QUERY_BLOCK) for blk in range(BLOCKS)
    ]
    rows = [slice(blk * QUERY_BLOCK, (blk + 1) * QUERY_BLOCK) for blk in range(BLOCKS)]
    windows = [
        pl.ds(blk * QUERY_BLOCK + REACH + offs[blk], KEY_WINDOW) for blk in range(BLOCKS)
    ]
    scores, limits, weights, mixes = {}, {}, {}, {}

    def score(blk):
        keys = k_s[windows[blk], :].astype(jnp.bfloat16)
        q = q_s[rows[blk], :]
        stacked = jnp.concatenate([q * m for m in head_ones], axis=0)
        biases = jnp.concatenate(
            [
                bias[rows[blk], h * KEY_WINDOW : (h + 1) * KEY_WINDOW]
                for h in range(HEADS)
            ],
            axis=0,
        )
        scores[blk] = lax.dot_general(
            jnp.concatenate([stacked, biases], axis=1),
            jnp.concatenate([keys, eye], axis=1),
            NT,
            preferred_element_type=jnp.float32,
        )
        place = tile * TILE + (blk * QUERY_BLOCK + PEN_OFF * 128) + offs[blk]
        turn = 128 - (place & 127)
        pair = pen_s[pl.ds(place >> 7, 2), :]
        turned = pltpu.roll(pair, turn & 127, 1)
        limits[blk] = jnp.where(lane < turn, turned[0:1], turned[1:2])

    def soften(blk):
        held = jnp.minimum(scores.pop(blk), limits.pop(blk))
        top = jnp.max(held, axis=1, keepdims=True)
        weights[blk] = jnp.exp(held - top).astype(jnp.bfloat16)

    def mix(blk):
        values = v_s[windows[blk], :].astype(jnp.bfloat16)
        mixes[blk] = dot(weights.pop(blk), jnp.concatenate([values, ones], axis=1))

    def finish(blk):
        mixed = mixes.pop(blk)
        num = mixed[0:QUERY_BLOCK, :C_ATOM]
        den = mixed[0:QUERY_BLOCK, C_ATOM:]
        for h in range(1, HEADS):
            part = mixed[h * QUERY_BLOCK : (h + 1) * QUERY_BLOCK]
            num = jnp.where(heads[h], part[:, :C_ATOM], num)
            den = jnp.where(heads[h], part[:, C_ATOM:], den)
        att_s[rows[blk], :] = (num / den * gate_s[rows[blk], :]).astype(jnp.bfloat16)

    for stage in (score, soften, mix, finish):
        for blk in range(BLOCKS):
            stage(blk)

    updated = (cur[...].astype(jnp.float32) + dot(att_s[...], wo[...])).astype(jnp.bfloat16)
    second = layer_norm(updated, g2[...])
    gated = dot(second, wfg[...])
    hidden = (gated * sigmoid(gated) * dot(second, wfu[...])).astype(jnp.bfloat16)
    atom_out = (updated.astype(jnp.float32) + dot(hidden, wfd[...])).astype(jnp.bfloat16)
    out[...] = atom_out

    @pl.when((step == 1) & has_right)
    def _():
        send_s[...] = out[...]
        tails[1].start()

    @pl.when((step == TILES - 1) & has_right)
    def _():
        for copy in tails:
            copy.wait_send()

    @pl.when((step == TILES - 1) & has_left)
    def _():
        for copy in tails:
            copy.wait_recv()


def attend(key_offsets, atoms, pair_bias, mask2, ids2, weights):
    per = TILE // REACH
    blocks = ATOM_DEV // REACH
    whole = lambda shape: pl.BlockSpec(shape, lambda t: (0,) * len(shape))
    anywhere = pl.BlockSpec(memory_space=pl.ANY)
    tiles = lambda width: pl.BlockSpec((TILE, width), lambda t: (tile_of(t), 0))
    in_specs = [
        pl.BlockSpec(memory_space=pltpu.SMEM),
        tiles(C_ATOM),
        pl.BlockSpec((REACH, C_ATOM), lambda t: (jnp.maximum(tile_of(t) * per - 1, 0), 0)),
        pl.BlockSpec((REACH, C_ATOM), lambda t: (jnp.minimum(tile_of(t) * per + per, blocks - 1), 0)),
        tiles(HEADS * KEY_WINDOW),
        whole(mask2.shape),
        pl.BlockSpec((FAR, 128), lambda t: (MASK_ROWS // FAR - 1, 0)),
        *[whole(w.shape) for w in weights],
        anywhere,
        anywhere,
    ]
    return pl.pallas_call(
        attention_kernel,
        grid=(TILES,),
        in_specs=in_specs,
        out_specs=[tiles(C_ATOM), anywhere, anywhere],
        out_shape=[
            jax.ShapeDtypeStruct((ATOM_DEV, C_ATOM), jnp.bfloat16),
            jax.ShapeDtypeStruct((DRIFT, C_ATOM), jnp.bfloat16),
            jax.ShapeDtypeStruct((FAR, 128), jnp.int32),
        ],
        scratch_shapes=[
            pltpu.VMEM((SPAN, C_ATOM), jnp.float32),
            pltpu.VMEM((SPAN, C_ATOM), jnp.float32),
            pltpu.VMEM((PEN_ROWS, 128), jnp.float32),
            pltpu.VMEM((TILE, C_ATOM), jnp.bfloat16),
            pltpu.VMEM((TILE, C_ATOM), jnp.float32),
            pltpu.VMEM((TILE, C_ATOM), jnp.bfloat16),
            pltpu.VMEM((DRIFT, C_ATOM), jnp.bfloat16),
            *[pltpu.VMEM((REACH, C_ATOM), jnp.bfloat16) for _ in range(4)],
            pltpu.VMEM((8, 128), jnp.int32),
            pltpu.VMEM((8, 128), jnp.int32),
            pltpu.VMEM((FAR, 128), jnp.int32),
            pltpu.SemaphoreType.DMA((6,)),
            pltpu.SemaphoreType.DMA((6,)),
        ],
        compiler_params=pltpu.CompilerParams(
            dimension_semantics=("arbitrary",),
            vmem_limit_bytes=VMEM_BYTES,
            collective_id=0,
            has_side_effects=True,
        ),
        cost_estimate=pl.CostEstimate(
            flops=6 * 10**9, bytes_accessed=14 * 2**20, transcendentals=6 * 10**6
        ),
    )(key_offsets, atoms, atoms, atoms, pair_bias, mask2, ids2, *weights, atoms, mask2)


def pool_kernel(
    tokens, ids_any, mask_any, marks_flat, marks_any, rows_any, far_any, wp_any, out, pooled,
    tok, far_tok, ids, mask, marks, rows, wp, acc_s, pooled_s, sems,
):
    me = here()
    base = me * TOK_DEV
    copies = [
        pltpu.make_async_copy(source, target, sems.at[i])
        for i, (source, target) in enumerate(
            [
                (wp_any, wp),
                (ids_any, ids),
                (mask_any, mask),
                (tokens, tok),
                *[
                    (rows_any.at[pl.ds(t * TILE, TILE)], rows.at[pl.ds(t * TILE, TILE)])
                    for t in range(TILES)
                ],
                (far_any, rows.at[pl.ds(ATOM_DEV, DRIFT)]),
                (marks_any, marks),
                (marks_flat, far_tok),
                (rows.at[pl.ds(0, ATOM_DEV)], out),
                *[
                    (pooled_s.at[pl.ds(i * WIN, WIN)], pooled.at[pl.ds(i * WIN, WIN)])
                    for i in range(TOK_DEV // WIN)
                ],
            ]
        )
    ]
    early, tiles, late = copies[:4], copies[4 : 4 + TILES], copies[4 + TILES : 7 + TILES]
    through, results = copies[7 + TILES], copies[8 + TILES :]
    for copy in [tiles[0], *early, *tiles[1:], *late]:
        copy.start()
    acc_s[...] = jnp.zeros(acc_s.shape, jnp.float32)
    for copy in early:
        copy.wait()
    slots = lax.broadcasted_iota(jnp.int32, (WIN, PART), 0)
    ones = jnp.ones((PART, 128), jnp.bfloat16)
    per = PART // 128

    def project(values):
        return jnp.maximum(dot(values, wp[...]), 0.0).astype(jnp.bfloat16)

    def window_sums(row, at, projected):
        table = (row - at == slots).astype(jnp.bfloat16)
        return dot(table, jnp.concatenate([projected, ones], axis=1))

    def part_of(local, head, tail):
        row = jnp.concatenate([local[i : i + 1] for i in range(per)], axis=1)
        start = jnp.clip(((head - base) >> 3) << 3, 0, TOK_DEV)
        end = jnp.minimum(tail - base, TOK_DEV - 1)
        return row, start, (jnp.maximum(end - start, 0) >> 7) + 1

    def own_part(part):
        at = slice(part * per, (part + 1) * per)
        local = jnp.where(mask[at, :] == 1, ids[at, :] - base, -1)
        return part_of(local, tok[part * PART], tok[part * PART + PART - 1])

    def far_part(part):
        mark = marks[part * per : (part + 1) * per, :]
        local = jnp.where(mark & 1 == 1, (mark >> 1) - base, -1)
        return part_of(local, far_tok[part * PART] >> 1, far_tok[part * PART + PART - 1] >> 1)

    def first_windows(parts, first_row):
        count = len(parts)
        projected = project(rows[first_row : first_row + count * PART, :])
        for i, (row, start, _) in enumerate(parts):
            at = pl.multiple_of(start, 8)
            acc_s[pl.ds(at, WIN), :] += window_sums(
                row, at, projected[i * PART : (i + 1) * PART]
            )

    def other_windows(parts, first_row):
        most = parts[0][2]
        for _, _, windows in parts[1:]:
            most = jnp.maximum(most, windows)

        @pl.when(most > 1)
        def _():
            for i, (row, start, windows) in enumerate(parts):
                at_row = first_row + i * PART

                @pl.when(windows > 1)
                def _(row=row, start=start, windows=windows, at_row=at_row):
                    projected = project(rows[at_row : at_row + PART, :])

                    def add(i, carry):
                        at = pl.multiple_of(start + i * WIN, 8)
                        acc_s[pl.ds(at, WIN), :] += window_sums(row, at, projected)
                        return carry

                    lax.fori_loop(1, windows, add, 0)

    own = [own_part(part) for part in range(ATOM_DEV // PART)]
    for t in range(TILES):
        tiles[t].wait()
        first_windows(own[t * TILE // PART : (t + 1) * TILE // PART], t * TILE)
    through.start()
    other_windows(own, 0)
    for copy in late:
        copy.wait()

    @pl.when(me > 0)
    def _():
        far = [far_part(part) for part in range(DRIFT // PART)]
        first_windows(far, ATOM_DEV)
        other_windows(far, ATOM_DEV)

    for i, copy in enumerate(results):
        at = slice(i * WIN, (i + 1) * WIN)
        counts = jnp.maximum(acc_s[at, C_TOKEN:], 1.0)
        pooled_s[at, :] = acc_s[at, :C_TOKEN] / jnp.concatenate(
            [counts] * (C_TOKEN // 128), axis=1
        )
        copy.start()
    for copy in [*results, through]:
        copy.wait()


def pool(tokens, ids2, mask2, far_marks, rows, far_rows, w_pool):
    anywhere = pl.BlockSpec(memory_space=pl.ANY)
    return pl.pallas_call(
        pool_kernel,
        in_specs=[anywhere] * 8,
        out_specs=[anywhere] * 2,
        out_shape=[
            jax.ShapeDtypeStruct((ATOM_DEV, C_ATOM), jnp.bfloat16),
            jax.ShapeDtypeStruct((TOK_DEV, C_TOKEN), jnp.float32),
        ],
        scratch_shapes=[
            pltpu.SMEM((ATOM_DEV,), jnp.int32),
            pltpu.SMEM((DRIFT,), jnp.int32),
            pltpu.VMEM((MASK_ROWS, 128), jnp.int32),
            pltpu.VMEM((MASK_ROWS, 128), jnp.int32),
            pltpu.VMEM((FAR, 128), jnp.int32),
            pltpu.VMEM((ATOM_DEV + DRIFT, C_ATOM), jnp.bfloat16),
            pltpu.VMEM((C_ATOM, C_TOKEN), jnp.bfloat16),
            pltpu.VMEM((ACC_ROWS, SUM_COLS), jnp.float32),
            pltpu.VMEM((TOK_DEV, C_TOKEN), jnp.float32),
            pltpu.SemaphoreType.DMA((8 + TILES + TOK_DEV // WIN,)),
        ],
        compiler_params=pltpu.CompilerParams(vmem_limit_bytes=VMEM_BYTES),
        cost_estimate=pl.CostEstimate(
            flops=5 * 10**9, bytes_accessed=8 * 2**20, transcendentals=0
        ),
    )(tokens, ids2, mask2, far_marks.reshape(-1), far_marks, rows, far_rows, w_pool)


def shards(
    atoms,
    pair_bias,
    key_offsets,
    atom_mask,
    atom_token,
    norm_gain,
    w_query,
    w_key,
    w_value,
    w_gate,
    w_out,
    trans_gain,
    w_ff_gate,
    w_ff_up,
    w_ff_down,
    w_pool,
):
    mask2 = atom_mask.reshape(MASK_ROWS, 128)
    ids2 = atom_token.reshape(MASK_ROWS, 128)
    weights = (
        norm_gain[None],
        w_query,
        w_key,
        w_value,
        w_gate,
        w_out,
        trans_gain[None],
        w_ff_gate,
        w_ff_up,
        w_ff_down,
    )
    rows, far_rows, far_marks = attend(key_offsets, atoms, pair_bias, mask2, ids2, weights)
    return tuple(pool(atom_token, ids2, mask2, far_marks, rows, far_rows, w_pool))


def solution(mesh):
    rows = P(("atom", "pair"))
    wide = P(("atom", "pair"), None)
    in_specs = (wide, wide, rows, rows, rows) + (P(),) * 11
    return jax.shard_map(
        shards, mesh=mesh, in_specs=in_specs, out_specs=(wide, wide), check_vma=False
    )
```

```python
import functools
import math

import jax
import jax.numpy as jnp
from jax import lax
from jax.experimental import pallas as pl
from jax.experimental.pallas import tpu as pltpu
from jax.sharding import PartitionSpec as P

C_ATOM = 128
HEADS = 4
HEAD = C_ATOM // HEADS
C_TOKEN = 384
QUERY_BLOCK = 32
KEY_WINDOW = 128
ATOM_DEV = 8192
REACH = 64
TOK_DEV = 1024
DRIFT = 2048
EPSILON = 1e-05
MASKED = -1000000000.0
LIVE = 3e38

TILE = DRIFT
BLOCKS = TILE // QUERY_BLOCK
SPAN = TILE + 2 * REACH
TILES = ATOM_DEV // TILE
PART = 512
WIN = 128
ACC_ROWS = TOK_DEV + WIN
SUM_COLS = C_TOKEN + 128
PEN_OFF = 8
MASK_ROWS = ATOM_DEV // 128
FAR = DRIFT // 128
END = 128
PEN_ROWS = MASK_ROWS + 2 * PEN_OFF
QSCALE = 1.0 / math.sqrt(HEAD)

NT = (((1,), (1,)), ((), ()))
AXES = ("atom", "pair")
MESH = pl.DeviceIdType.MESH
VMEM_BYTES = 60 * 1024 * 1024


def dot(a, b):
    return jnp.dot(a, b, preferred_element_type=jnp.float32)


def layer_norm(rows, gain):
    same = lax.broadcasted_iota(jnp.int32, (C_ATOM, C_ATOM), 0) == lax.broadcasted_iota(
        jnp.int32, (C_ATOM, C_ATOM), 1
    )
    share = 1.0 / C_ATOM
    centering = jnp.where(same, 1.0 - share, -share).astype(jnp.bfloat16)
    center = dot(rows, centering)
    averaging = jnp.full((C_ATOM, C_ATOM), share, jnp.bfloat16)
    spread = dot((center * center).astype(jnp.bfloat16), averaging)
    return (center * lax.rsqrt(spread + EPSILON) * gain).astype(jnp.bfloat16)


def sigmoid(x):
    return 0.5 * jnp.tanh(0.5 * x) + 0.5


def tile_of(step):
    return jnp.where(step == 0, 3, jnp.where(step == 3, 0, step))


def here():
    return lax.axis_index("atom") * lax.axis_size("pair") + lax.axis_index("pair")


def place_of(device):
    pair = lax.axis_size("pair")
    return (device // pair, device % pair)


def attention_kernel(
    koff, cur, prev, nxt, bias, mask, ids, end_rows, near_end, end_bias,
    g1, wq, wk, wv, wg, wo, g2, wfg, wfu, wfd,
    atoms_any, mask_any,
    out, end_out, got_rows, got_marks,
    k_s, v_s, pen_s, q_s, gate_s, att_s, send_s, send_end, low, high, below, above,
    below_mask, above_mask, marks_s, send_sem, recv_sem,
):
    step = pl.program_id(0)
    tile = tile_of(step)
    me = here()
    devices = lax.axis_size("atom") * lax.axis_size("pair")
    right = place_of((me + 1) % devices)
    left = place_of((me + devices - 1) % devices)

    def remote(source, target, n, device):
        return pltpu.make_async_remote_copy(
            src_ref=source,
            dst_ref=target,
            send_sem=send_sem.at[n],
            recv_sem=recv_sem.at[n],
            device_id=device,
            device_id_type=MESH,
        )

    ups = [
        remote(atoms_any.at[pl.ds(ATOM_DEV - REACH, REACH)], below, 0, right),
        remote(mask_any.at[pl.ds(MASK_ROWS - 8, 8)], below_mask, 2, right),
    ]
    downs = [
        remote(atoms_any.at[pl.ds(0, REACH)], above, 1, left),
        remote(mask_any.at[pl.ds(0, 8)], above_mask, 3, left),
    ]
    main = pl.ds(0, DRIFT - END)
    tails = [
        remote(marks_s, got_marks, 4, right),
        remote(send_s.at[main], got_rows.at[main], 5, right),
        remote(send_end, got_rows.at[pl.ds(DRIFT - END, END)], 6, right),
    ]
    has_right, has_left = me < devices - 1, me > 0

    @pl.when(step == 0)
    def _():
        barrier = pltpu.get_barrier_semaphore()

        @pl.when(has_right)
        def _():
            pl.semaphore_signal(barrier, inc=1, device_id=right, device_id_type=MESH)

        @pl.when(has_left)
        def _():
            pl.semaphore_signal(barrier, inc=1, device_id=left, device_id_type=MESH)

        pen_s[PEN_OFF : PEN_OFF + MASK_ROWS, :] = jnp.where(mask[...] == 1, LIVE, MASKED)
        nothing = jnp.full((PEN_OFF, 128), MASKED, jnp.float32)
        pen_s[0:PEN_OFF, :] = nothing
        pen_s[PEN_ROWS - PEN_OFF :, :] = nothing
        low[...] = jnp.zeros((REACH, C_ATOM), jnp.bfloat16)
        high[...] = jnp.zeros((REACH, C_ATOM), jnp.bfloat16)
        marks_s[...] = ids[...] * 2 + mask[MASK_ROWS - FAR :, :]

    lane = lax.broadcasted_iota(jnp.int32, (1, C_ATOM), 1)
    heads = [(lane // HEAD == h) for h in range(HEADS)]
    head_ones = [m.astype(jnp.bfloat16) for m in heads]
    eye = (
        lax.broadcasted_iota(jnp.int32, (KEY_WINDOW, KEY_WINDOW), 0)
        == lax.broadcasted_iota(jnp.int32, (KEY_WINDOW, KEY_WINDOW), 1)
    ).astype(jnp.bfloat16)
    ones = jnp.ones((KEY_WINDOW, 128), jnp.bfloat16)

    def block_out(rows_in, bias_ref, row0, count):
        blocks = count // QUERY_BLOCK
        middle = rows_in[REACH : REACH + count]
        normed = layer_norm(rows_in, g1[...])
        kv = dot(normed, jnp.concatenate([wk[...], wv[...]], axis=1))
        k_s[0 : count + 2 * REACH, :] = kv[:, :C_ATOM]
        v_s[0 : count + 2 * REACH, :] = kv[:, C_ATOM:]
        qg = dot(normed[REACH : REACH + count], jnp.concatenate([wq[...], wg[...]], axis=1))
        q_s[0:count, :] = (qg[:, :C_ATOM] * QSCALE).astype(jnp.bfloat16)
        gate_s[0:count, :] = sigmoid(qg[:, C_ATOM:])

        offs = [
            jnp.clip(koff[row0 // QUERY_BLOCK + blk], -REACH, -QUERY_BLOCK) for blk in range(blocks)
        ]
        rows = [slice(blk * QUERY_BLOCK, (blk + 1) * QUERY_BLOCK) for blk in range(blocks)]
        windows = [
            pl.ds(blk * QUERY_BLOCK + REACH + offs[blk], KEY_WINDOW) for blk in range(blocks)
        ]
        scores, limits, weights, mixes = {}, {}, {}, {}

        def score(blk):
            keys = k_s[windows[blk], :].astype(jnp.bfloat16)
            q = q_s[rows[blk], :]
            stacked = jnp.concatenate([q * m for m in head_ones], axis=0)
            biases = jnp.concatenate(
                [
                    bias_ref[rows[blk], h * KEY_WINDOW : (h + 1) * KEY_WINDOW]
                    for h in range(HEADS)
                ],
                axis=0,
            )
            scores[blk] = lax.dot_general(
                jnp.concatenate([stacked, biases], axis=1),
                jnp.concatenate([keys, eye], axis=1),
                NT,
                preferred_element_type=jnp.float32,
            )
            place = row0 + (blk * QUERY_BLOCK + PEN_OFF * 128) + offs[blk]
            turn = 128 - (place & 127)
            pair = pen_s[pl.ds(place >> 7, 2), :]
            turned = pltpu.roll(pair, turn & 127, 1)
            limits[blk] = jnp.where(lane < turn, turned[0:1], turned[1:2])

        def soften(blk):
            held = jnp.minimum(scores.pop(blk), limits.pop(blk))
            top = jnp.max(held, axis=1, keepdims=True)
            weights[blk] = jnp.exp(held - top).astype(jnp.bfloat16)

        def mix(blk):
            values = v_s[windows[blk], :].astype(jnp.bfloat16)
            mixes[blk] = dot(weights.pop(blk), jnp.concatenate([values, ones], axis=1))

        def finish(blk):
            mixed = mixes.pop(blk)
            num = mixed[0:QUERY_BLOCK, :C_ATOM]
            den = mixed[0:QUERY_BLOCK, C_ATOM:]
            for h in range(1, HEADS):
                part = mixed[h * QUERY_BLOCK : (h + 1) * QUERY_BLOCK]
                num = jnp.where(heads[h], part[:, :C_ATOM], num)
                den = jnp.where(heads[h], part[:, C_ATOM:], den)
            att_s[rows[blk], :] = (num / den * gate_s[rows[blk], :]).astype(jnp.bfloat16)

        for stage in (score, soften, mix, finish):
            for blk in range(blocks):
                stage(blk)

        mixed = dot(att_s[0:count, :], wo[...])
        updated = (middle.astype(jnp.float32) + mixed).astype(jnp.bfloat16)
        second = layer_norm(updated, g2[...])
        gated = dot(second, wfg[...])
        hidden = (gated * sigmoid(gated) * dot(second, wfu[...])).astype(jnp.bfloat16)
        return (updated.astype(jnp.float32) + dot(hidden, wfd[...])).astype(jnp.bfloat16)

    first = jnp.where(tile == 0, low[...], prev[...])
    last = jnp.where(tile == TILES - 1, high[...], nxt[...])
    rows_in = jnp.concatenate([first, cur[...], last], axis=0)
    out[...] = block_out(rows_in, bias, tile * TILE, TILE)

    @pl.when(step == 0)
    def _():
        barrier = pltpu.get_barrier_semaphore()
        pl.semaphore_wait(barrier, has_right.astype(jnp.int32) + has_left.astype(jnp.int32))

        @pl.when(has_right)
        def _():
            for copy in ups:
                copy.start()
            send_s[...] = out[...]
            for copy in tails[:2]:
                copy.start()

        @pl.when(has_left)
        def _():
            for copy in downs:
                copy.start()

    @pl.when(step == 1)
    def _():
        @pl.when(has_left)
        def _():
            for copy in ups:
                copy.wait_recv()
            low[...] = below[...]
            pen_s[0:PEN_OFF, :] = jnp.where(below_mask[...] == 1, LIVE, MASKED)
            for copy in downs:
                copy.wait_send()

        @pl.when(has_right)
        def _():
            for copy in downs:
                copy.wait_recv()
            high[...] = above[...]
            pen_s[PEN_ROWS - PEN_OFF :, :] = jnp.where(above_mask[...] == 1, LIVE, MASKED)
            for copy in ups:
                copy.wait_send()

    @pl.when(step == 1)
    def _():
        rows_in = jnp.concatenate([near_end[...], end_rows[...], high[...]], axis=0)
        send_end[...] = block_out(rows_in, end_bias, ATOM_DEV - END, END)
        end_out[...] = send_end[...]

        @pl.when(has_right)
        def _():
            tails[2].start()

    @pl.when((step == TILES - 1) & has_right)
    def _():
        for copy in tails:
            copy.wait_send()

    @pl.when((step == TILES - 1) & has_left)
    def _():
        for copy in tails:
            copy.wait_recv()


def attend(key_offsets, atoms, pair_bias, mask2, ids2, weights):
    per = TILE // REACH
    blocks = ATOM_DEV // REACH
    whole = lambda shape: pl.BlockSpec(shape, lambda t: (0,) * len(shape))
    anywhere = pl.BlockSpec(memory_space=pl.ANY)
    tiles = lambda width: pl.BlockSpec((TILE, width), lambda t: (tile_of(t), 0))
    in_specs = [
        pl.BlockSpec(memory_space=pltpu.SMEM),
        tiles(C_ATOM),
        pl.BlockSpec((REACH, C_ATOM), lambda t: (jnp.maximum(tile_of(t) * per - 1, 0), 0)),
        pl.BlockSpec((REACH, C_ATOM), lambda t: (jnp.minimum(tile_of(t) * per + per, blocks - 1), 0)),
        tiles(HEADS * KEY_WINDOW),
        whole(mask2.shape),
        pl.BlockSpec((FAR, 128), lambda t: (MASK_ROWS // FAR - 1, 0)),
        pl.BlockSpec((END, C_ATOM), lambda t: (ATOM_DEV // END - 1, 0)),
        pl.BlockSpec((REACH, C_ATOM), lambda t: ((ATOM_DEV - END) // REACH - 1, 0)),
        pl.BlockSpec((END, HEADS * KEY_WINDOW), lambda t: (ATOM_DEV // END - 1, 0)),
        *[whole(w.shape) for w in weights],
        anywhere,
        anywhere,
    ]
    return pl.pallas_call(
        attention_kernel,
        grid=(TILES,),
        in_specs=in_specs,
        out_specs=[tiles(C_ATOM), whole((END, C_ATOM)), anywhere, anywhere],
        out_shape=[
            jax.ShapeDtypeStruct((ATOM_DEV, C_ATOM), jnp.bfloat16),
            jax.ShapeDtypeStruct((END, C_ATOM), jnp.bfloat16),
            jax.ShapeDtypeStruct((DRIFT, C_ATOM), jnp.bfloat16),
            jax.ShapeDtypeStruct((FAR, 128), jnp.int32),
        ],
        scratch_shapes=[
            pltpu.VMEM((SPAN, C_ATOM), jnp.float32),
            pltpu.VMEM((SPAN, C_ATOM), jnp.float32),
            pltpu.VMEM((PEN_ROWS, 128), jnp.float32),
            pltpu.VMEM((TILE, C_ATOM), jnp.bfloat16),
            pltpu.VMEM((TILE, C_ATOM), jnp.float32),
            pltpu.VMEM((TILE, C_ATOM), jnp.bfloat16),
            pltpu.VMEM((DRIFT, C_ATOM), jnp.bfloat16),
            pltpu.VMEM((END, C_ATOM), jnp.bfloat16),
            *[pltpu.VMEM((REACH, C_ATOM), jnp.bfloat16) for _ in range(4)],
            pltpu.VMEM((8, 128), jnp.int32),
            pltpu.VMEM((8, 128), jnp.int32),
            pltpu.VMEM((FAR, 128), jnp.int32),
            pltpu.SemaphoreType.DMA((7,)),
            pltpu.SemaphoreType.DMA((7,)),
        ],
        compiler_params=pltpu.CompilerParams(
            dimension_semantics=("arbitrary",),
            vmem_limit_bytes=VMEM_BYTES,
            collective_id=0,
            has_side_effects=True,
        ),
        cost_estimate=pl.CostEstimate(
            flops=6 * 10**9, bytes_accessed=14 * 2**20, transcendentals=6 * 10**6
        ),
    )(key_offsets, atoms, atoms, atoms, pair_bias, mask2, ids2, atoms, atoms, pair_bias, *weights, atoms, mask2)


def pool_kernel(
    tokens, ids_any, mask_any, marks_flat, marks_any, rows_any, end_any, far_any, wp_any, out, pooled,
    tok, far_tok, ids, mask, marks, rows, wp, acc_s, pooled_s, sems,
):
    me = here()
    base = me * TOK_DEV
    copies = [
        pltpu.make_async_copy(source, target, sems.at[i])
        for i, (source, target) in enumerate(
            [
                (wp_any, wp),
                (ids_any, ids),
                (mask_any, mask),
                (tokens, tok),
                *[
                    (rows_any.at[pl.ds(t * TILE, size)], rows.at[pl.ds(t * TILE, size)])
                    for t, size in enumerate([TILE] * (TILES - 1) + [TILE - END])
                ],
                (end_any, rows.at[pl.ds(ATOM_DEV - END, END)]),
                (far_any, rows.at[pl.ds(ATOM_DEV, DRIFT)]),
                (marks_any, marks),
                (marks_flat, far_tok),
                (rows.at[pl.ds(0, ATOM_DEV)], out),
                *[
                    (pooled_s.at[pl.ds(i * WIN, WIN)], pooled.at[pl.ds(i * WIN, WIN)])
                    for i in range(TOK_DEV // WIN)
                ],
            ]
        )
    ]
    early, tiles, end = copies[:4], copies[4 : 4 + TILES], copies[4 + TILES]
    late, through, results = copies[5 + TILES : 8 + TILES], copies[8 + TILES], copies[9 + TILES :]
    for copy in [tiles[0], *early, *tiles[1:], end, *late]:
        copy.start()
    acc_s[...] = jnp.zeros(acc_s.shape, jnp.float32)
    for copy in early:
        copy.wait()
    slots = lax.broadcasted_iota(jnp.int32, (WIN, PART), 0)
    ones = jnp.ones((PART, 128), jnp.bfloat16)
    per = PART // 128

    def project(values):
        return jnp.maximum(dot(values, wp[...]), 0.0).astype(jnp.bfloat16)

    def window_sums(row, at, projected):
        table = (row - at == slots).astype(jnp.bfloat16)
        return dot(table, jnp.concatenate([projected, ones], axis=1))

    def part_of(local, head, tail):
        row = jnp.concatenate([local[i : i + 1] for i in range(per)], axis=1)
        start = jnp.clip(((head - base) >> 3) << 3, 0, TOK_DEV)
        end = jnp.minimum(tail - base, TOK_DEV - 1)
        return row, start, (jnp.maximum(end - start, 0) >> 7) + 1

    def own_part(part):
        at = slice(part * per, (part + 1) * per)
        local = jnp.where(mask[at, :] == 1, ids[at, :] - base, -1)
        return part_of(local, tok[part * PART], tok[part * PART + PART - 1])

    def far_part(part):
        mark = marks[part * per : (part + 1) * per, :]
        local = jnp.where(mark & 1 == 1, (mark >> 1) - base, -1)
        return part_of(local, far_tok[part * PART] >> 1, far_tok[part * PART + PART - 1] >> 1)

    def first_windows(parts, first_row):
        count = len(parts)
        projected = project(rows[first_row : first_row + count * PART, :])
        for i, (row, start, _) in enumerate(parts):
            at = pl.multiple_of(start, 8)
            acc_s[pl.ds(at, WIN), :] += window_sums(
                row, at, projected[i * PART : (i + 1) * PART]
            )

    def other_windows(parts, first_row):
        most = parts[0][2]
        for _, _, windows in parts[1:]:
            most = jnp.maximum(most, windows)

        @pl.when(most > 1)
        def _():
            for i, (row, start, windows) in enumerate(parts):
                at_row = first_row + i * PART

                @pl.when(windows > 1)
                def _(row=row, start=start, windows=windows, at_row=at_row):
                    projected = project(rows[at_row : at_row + PART, :])

                    def add(i, carry):
                        at = pl.multiple_of(start + i * WIN, 8)
                        acc_s[pl.ds(at, WIN), :] += window_sums(row, at, projected)
                        return carry

                    lax.fori_loop(1, windows, add, 0)

    own = [own_part(part) for part in range(ATOM_DEV // PART)]
    for t in range(TILES):
        tiles[t].wait()
        if t == TILES - 1:
            end.wait()
        first_windows(own[t * TILE // PART : (t + 1) * TILE // PART], t * TILE)
    through.start()
    other_windows(own, 0)
    for copy in late:
        copy.wait()

    @pl.when(me > 0)
    def _():
        far = [far_part(part) for part in range(DRIFT // PART)]
        first_windows(far, ATOM_DEV)
        other_windows(far, ATOM_DEV)

    for i, copy in enumerate(results):
        at = slice(i * WIN, (i + 1) * WIN)
        counts = jnp.maximum(acc_s[at, C_TOKEN:], 1.0)
        pooled_s[at, :] = acc_s[at, :C_TOKEN] / jnp.concatenate(
            [counts] * (C_TOKEN // 128), axis=1
        )
        copy.start()
    for copy in [*results, through]:
        copy.wait()


def pool(tokens, ids2, mask2, far_marks, rows, end_rows, far_rows, w_pool):
    anywhere = pl.BlockSpec(memory_space=pl.ANY)
    return pl.pallas_call(
        pool_kernel,
        in_specs=[anywhere] * 9,
        out_specs=[anywhere] * 2,
        out_shape=[
            jax.ShapeDtypeStruct((ATOM_DEV, C_ATOM), jnp.bfloat16),
            jax.ShapeDtypeStruct((TOK_DEV, C_TOKEN), jnp.float32),
        ],
        scratch_shapes=[
            pltpu.SMEM((ATOM_DEV,), jnp.int32),
            pltpu.SMEM((DRIFT,), jnp.int32),
            pltpu.VMEM((MASK_ROWS, 128), jnp.int32),
            pltpu.VMEM((MASK_ROWS, 128), jnp.int32),
            pltpu.VMEM((FAR, 128), jnp.int32),
            pltpu.VMEM((ATOM_DEV + DRIFT, C_ATOM), jnp.bfloat16),
            pltpu.VMEM((C_ATOM, C_TOKEN), jnp.bfloat16),
            pltpu.VMEM((ACC_ROWS, SUM_COLS), jnp.float32),
            pltpu.VMEM((TOK_DEV, C_TOKEN), jnp.float32),
            pltpu.SemaphoreType.DMA((9 + TILES + TOK_DEV // WIN,)),
        ],
        compiler_params=pltpu.CompilerParams(vmem_limit_bytes=VMEM_BYTES),
        cost_estimate=pl.CostEstimate(
            flops=5 * 10**9, bytes_accessed=8 * 2**20, transcendentals=0
        ),
    )(tokens, ids2, mask2, far_marks.reshape(-1), far_marks, rows, end_rows, far_rows, w_pool)


def shards(
    atoms,
    pair_bias,
    key_offsets,
    atom_mask,
    atom_token,
    norm_gain,
    w_query,
    w_key,
    w_value,
    w_gate,
    w_out,
    trans_gain,
    w_ff_gate,
    w_ff_up,
    w_ff_down,
    w_pool,
):
    mask2 = atom_mask.reshape(MASK_ROWS, 128)
    ids2 = atom_token.reshape(MASK_ROWS, 128)
    weights = (
        norm_gain[None],
        w_query,
        w_key,
        w_value,
        w_gate,
        w_out,
        trans_gain[None],
        w_ff_gate,
        w_ff_up,
        w_ff_down,
    )
    rows, end_rows, far_rows, far_marks = attend(key_offsets, atoms, pair_bias, mask2, ids2, weights)
    return tuple(pool(atom_token, ids2, mask2, far_marks, rows, end_rows, far_rows, w_pool))


def solution(mesh):
    rows = P(("atom", "pair"))
    wide = P(("atom", "pair"), None)
    in_specs = (wide, wide, rows, rows, rows) + (P(),) * 11
    return jax.shard_map(
        shards, mesh=mesh, in_specs=in_specs, out_specs=(wide, wide), check_vma=False
    )
```
